512 devices in a mesh: dp: 32 (over x, y, core), fsdp: 16 (over z).
Axes of the slice: x: 4, y: 4, z: 16, core: 2. Of those that a mesh axis runs over, the one named last changes fastest.
Arguments:
- patches: bfloat16 [32, 16, 3, 80, 1280], P('dp', 'fsdp'), may hold values from -16 to 16
- counts: int32 [32, 16, 3], P('dp', 'fsdp'), may hold values from 0 to 80, as said below
- norm_gain: float32 [1280], replicated, may hold values from 0.25 to 1.75
- norm_bias: float32 [1280], replicated, may hold values from -1.75 to 1.75
- input_weight: bfloat16 [1280, 1920], P('fsdp'), may hold values from -5 to 5
- latent_query: bfloat16 [64, 640], replicated, may hold values from -16 to 16
- cotangent: bfloat16 [32, 16, 3, 64, 640], P('dp', 'fsdp'), may hold values from -0.0390625 to 0.0390625
Outputs:
- latents: float32 [32, 16, 3, 64, 640], P('dp', 'fsdp')
- grad_value: float32 [1280, 640], P('fsdp')
The draws below stay inside these ranges and needn't reach their ends.
Inputs may be any that keep to these rules, and one draw needn't show every extreme that they name: `counts`: A device holds its images in its first slots, each with 64 to 80 patches, and count 0 in the slots after them; it holds 1 to 3 images, and the devices of one fsdp index hold 2 times the dp axis's size images in all. Some device holds exactly 3 images and some image has exactly 80 patches.
All inputs are finite; a program needn't handle non-finite values.
Results may differ from the reference program's by a relative error of at most 0.012.
The reference program's roundings to bfloat16 on the way count: a program that leaves them out, or rounds other values in their place, can miss the bound.
Values may be sent and summed in bfloat16 or wider, within the bound.
No kernel may reach another device: no remote copies, remote signals or barrier semaphores. Data moves between devices by JAX's collectives and lax.ppermute only.
A program may use at most 64 MiB of HBM per device.

```python
import math
import jax
import jax.numpy as jnp
from jax import lax

D = 1280
HEADS = 8
HEAD_DIM = 80
LATENTS = 64
PATCH_MAX = 80
IMAGES = 2
IMAGES_MAX = 3
INNER = 640
N_DP = 32
N_FSDP = 16


def draw_counts(key, part):
    key = jax.random.fold_in(key, 11)
    keys = jax.random.split(key, 4)
    half = N_DP // 2
    extra = jax.random.randint(keys[0], (N_FSDP, half), 0, IMAGES)
    extra = extra.at[:, 0].set(IMAGES_MAX - IMAGES)
    paired = jnp.concatenate([IMAGES + extra, IMAGES - extra], axis=1)
    orders = jax.vmap(lambda single: jax.random.permutation(single, N_DP))(jax.random.split(keys[1], N_FSDP))
    owned = jnp.take_along_axis(paired, orders, axis=1)
    sizes = jax.random.randint(keys[2], (N_DP, N_FSDP, IMAGES_MAX), PATCH_MAX * 4 // 5, PATCH_MAX + 1)
    chosen = jax.random.randint(keys[3], (N_FSDP,), 0, N_DP)
    sizes = sizes.at[chosen, jnp.arange(N_FSDP), 0].set(PATCH_MAX)
    slot_ids = jnp.arange(IMAGES_MAX)
    live = slot_ids[None, None, :] < owned.T[:, :, None]
    return jnp.where(live, sizes, 0).astype(jnp.int32)


def draw_patches(key, part):
    key = jax.random.fold_in(key, 23)
    first = jax.random.fold_in(key, 0)
    shape = (N_DP, N_FSDP, IMAGES_MAX, PATCH_MAX, D)
    return jnp.clip(jax.random.normal(first, shape, jnp.float32), -6.0, 6.0).astype(jnp.bfloat16)


def draw_input_weight(key, part):
    key = jax.random.fold_in(key, 37)
    first = jax.random.fold_in(key, 0)
    base = jnp.clip(jax.random.normal(first, (D, 3 * HEADS * HEAD_DIM), jnp.float32), -5.0, 5.0) * D ** (-0.5)
    return base.astype(jnp.bfloat16)


def draw_latent_query(key, part):
    key = jax.random.fold_in(key, 53)
    first = jax.random.fold_in(key, 0)
    shape = (LATENTS, HEADS * HEAD_DIM)
    return jnp.clip(jax.random.normal(first, shape, jnp.float32), -5.0, 5.0).astype(jnp.bfloat16)


def block_scale(key, shape, cuts, smallest, largest):
    factor_of = 1.0
    for position, blocks in cuts:
        heights = jax.random.uniform(jax.random.fold_in(jax.random.fold_in(key, 6), position), (blocks,), jnp.float32, smallest / len(cuts), largest / len(cuts))
        factor_of = factor_of * jnp.repeat(jnp.exp(heights), shape[position] // blocks).reshape((-1,) + (1,) * (len(shape) - 1 - position))
    return factor_of


def scatter_about(rng, shape, scale, reach, pieces=(), kind=jnp.bfloat16):
    loudness = block_scale(rng, shape, pieces, -0.22, 0.18) if pieces else 1.0
    array = jax.random.normal(rng, shape, jnp.float32) * scale * loudness
    return jnp.minimum(jnp.maximum(array, -reach), reach).astype(kind)


def setup_inputs(seed: int = 0) -> dict:
    streams_of = jax.random.split(jax.random.key(seed), 8)
    return {
        "patches": draw_patches(jax.random.fold_in(streams_of[7], 71), 0),
        "counts": draw_counts(jax.random.fold_in(streams_of[7], 71), 0),
        "norm_gain": jnp.clip(1.0 + 0.15 * jax.random.normal(streams_of[2], (D,), jnp.float32), 0.25, 1.75),
        "norm_bias": scatter_about(streams_of[3], (D,), 0.3, 1.75, (), jnp.float32),
        "input_weight": draw_input_weight(jax.random.fold_in(streams_of[7], 71), 0),
        "latent_query": draw_latent_query(jax.random.fold_in(streams_of[7], 71), 0),
        "cotangent": scatter_about(streams_of[6], (N_DP, N_FSDP, IMAGES_MAX, LATENTS, INNER), (2 * (N_DP * N_FSDP * IMAGES * PATCH_MAX) ** -0.5), 0.0390625, ((0, 32), (1, 16))),
    }


EPSILON = 1e-06
MASKED = -1e+30

def product(form, left, right):
    return jnp.einsum(form, left.astype(jnp.float32), right.astype(jnp.float32), precision=lax.Precision.HIGHEST)

def layer_norm(rows, gain, bias):
    values = rows.astype(jnp.float32)
    centre = values - lax.optimization_barrier(jnp.mean(values, axis=-1, keepdims=True))
    spread = lax.optimization_barrier(jnp.mean(centre * centre, axis=-1, keepdims=True))
    return (centre * lax.rsqrt(spread + EPSILON) * gain + bias).astype(jnp.bfloat16)

def forward_window(projected, segment, groups, kinds, latent_query):
    width = projected.shape[1] // 3
    head_size = width // HEADS
    span = projected.shape[0] // groups
    scale = 1.0 / math.sqrt(head_size)
    parts = projected.astype(jnp.bfloat16).reshape(groups, span, 3, HEADS, head_size)
    queries = parts[:, :, 0]
    keys = parts[:, :, 1]
    values = parts[:, :, 2]
    labels = segment.reshape(groups, span)
    valid = labels < kinds
    allowed = ((labels[:, :, None] == labels[:, None, :]) & valid[:, :, None])[:, None]
    scores = jnp.where(allowed, product('gqhd,gchd->ghqc', queries, keys) * scale, MASKED)
    raised = jnp.where(allowed, jnp.exp(scores - lax.optimization_barrier(jnp.max(scores, axis=-1, keepdims=True))), 0.0)
    weights = (raised / jnp.maximum(lax.optimization_barrier(jnp.sum(raised, axis=-1, keepdims=True)), 1.0)).astype(jnp.bfloat16)
    mixed = product('ghqc,gchd->gqhd', weights, values).astype(jnp.bfloat16)
    member = labels[:, None, :] == jnp.arange(kinds, dtype=jnp.int32)[None, :, None]
    latent_wide = latent_query.reshape(latent_query.shape[0], HEADS, head_size)
    latent_scores = product('lhd,grhd->ghlr', latent_wide, mixed) * scale
    inside = member[:, None, None]
    masked = jnp.where(inside, latent_scores[:, :, :, None, :], MASKED)
    raised_latent = jnp.where(inside, jnp.exp(masked - lax.optimization_barrier(jnp.max(masked, axis=-1, keepdims=True))), 0.0)
    shares = raised_latent / jnp.maximum(lax.optimization_barrier(jnp.sum(raised_latent, axis=-1, keepdims=True)), 1.0)
    shares_low = shares.astype(jnp.bfloat16)
    latents = product('ghlkr,grhd->gklhd', shares_low, mixed).astype(jnp.float32)
    return (latents.reshape(groups * kinds, latent_query.shape[0], width), (weights, mixed, shares, shares_low))

def backward_window(saved, grads, groups, kinds, latent_query):
    weights, mixed, shares, shares_low = saved
    width = latent_query.shape[1]
    head_size = width // HEADS
    count_latent = latent_query.shape[0]
    scale = 1.0 / math.sqrt(head_size)
    grad_blocks = grads.reshape(groups, kinds, count_latent, HEADS, head_size)
    share_grads = product('gklhd,grhd->ghlkr', grad_blocks, mixed)
    centre = lax.optimization_barrier(jnp.sum(shares * share_grads, axis=-1, keepdims=True))
    score_grads = shares * (share_grads - centre) * scale
    from_values = product('ghlkr,gklhd->grhd', shares_low, grad_blocks)
    from_keys = product('ghlkr,lhd->grhd', score_grads, latent_query.reshape(count_latent, HEADS, head_size))
    mixed_grad = (from_values + from_keys).astype(jnp.bfloat16)
    value_grad = product('ghqc,gqhd->gchd', weights, mixed_grad).astype(jnp.bfloat16)
    return value_grad.reshape(groups * value_grad.shape[1], width)

def reference(patches, counts, norm_gain, norm_bias, input_weight, latent_query, cotangent):
    owners = N_DP * N_FSDP
    images = patches.reshape(owners, IMAGES_MAX, PATCH_MAX, D)
    sizes = counts.reshape(owners, IMAGES_MAX)
    grads = cotangent.reshape(owners, IMAGES_MAX, LATENTS, INNER)
    offsets = jnp.arange(PATCH_MAX, dtype=jnp.int32)

    def one_owner(total, item):
        block, slot_sizes, grad_block = item
        labels = jnp.where(offsets[None, :] < slot_sizes[:, None], 0, 1).astype(jnp.int32).reshape(IMAGES_MAX * PATCH_MAX)
        normed = layer_norm(block.reshape(IMAGES_MAX * PATCH_MAX, D), norm_gain, norm_bias)
        projected = jnp.dot(normed, input_weight, preferred_element_type=jnp.float32)
        latents, saved = forward_window(projected, labels, IMAGES_MAX, 1, latent_query)
        value_grad = backward_window(saved, grad_block, IMAGES_MAX, 1, latent_query)
        return (total + product('rd,rv->dv', normed, value_grad), latents)
    grad_value, latents = lax.scan(one_owner, jnp.zeros((D, INNER), jnp.float32), (images, sizes, grads))
    return (latents.reshape(N_DP, N_FSDP, IMAGES_MAX, LATENTS, INNER), grad_value)
```

```python
import math

import jax
import jax.numpy as jnp
from jax import lax
from jax.sharding import Mesh
from jax.sharding import PartitionSpec as P

HEADS = 2
EPSILON = 1e-06
MASKED = -1e30
DP = ("xp", "xi", "y", "c")
PLANE = ("xp", "y")
SWAP = [(0, 1), (1, 0)]


def layer_norm(rows, gain, bias):
    values = rows.astype(jnp.float32)
    centre = values - jnp.mean(values, axis=-1, keepdims=True)
    spread = jnp.mean(centre * centre, axis=-1, keepdims=True)
    return (centre * lax.rsqrt(spread + EPSILON) * gain + bias).astype(jnp.bfloat16)


def forward_window(projected, sizes, latent_query):
    groups = sizes.shape[0]
    width = projected.shape[1] // 3
    head_size = width // HEADS
    span = projected.shape[0] // groups
    scale = 1.0 / math.sqrt(head_size)
    parts = projected.astype(jnp.bfloat16).reshape(groups, span, 3, HEADS, head_size)
    queries, keys, values = parts[:, :, 0], parts[:, :, 1], parts[:, :, 2]
    valid = jnp.arange(span, dtype=jnp.int32)[None, :] < sizes[:, None]
    allowed = (valid[:, :, None] & valid[:, None, :])[:, None]
    scores = (
        jnp.einsum("gqhd,gchd->ghqc", queries, keys, preferred_element_type=jnp.float32) * scale
    )
    scores = jnp.where(allowed, scores, MASKED)
    raised = jnp.where(allowed, jnp.exp(scores - jnp.max(scores, axis=-1, keepdims=True)), 0.0)
    weights = (raised / jnp.maximum(jnp.sum(raised, axis=-1, keepdims=True), 1.0)).astype(
        jnp.bfloat16
    )
    mixed = jnp.einsum(
        "ghqc,gchd->gqhd", weights, values, preferred_element_type=jnp.float32
    ).astype(jnp.bfloat16)
    latent_wide = latent_query.reshape(latent_query.shape[0], HEADS, head_size)
    latent_scores = (
        jnp.einsum("lhd,grhd->ghlr", latent_wide, mixed, preferred_element_type=jnp.float32) * scale
    )
    inside = valid[:, None, None, :]
    masked = jnp.where(inside, latent_scores, MASKED)
    raised_latent = jnp.where(
        inside, jnp.exp(masked - jnp.max(masked, axis=-1, keepdims=True)), 0.0
    )
    shares = raised_latent / jnp.maximum(jnp.sum(raised_latent, axis=-1, keepdims=True), 1.0)
    shares_low = shares.astype(jnp.bfloat16)
    latents = jnp.einsum("ghlr,grhd->glhd", shares_low, mixed, preferred_element_type=jnp.float32)
    return (
        latents.reshape(groups, latent_query.shape[0], width),
        (weights, mixed, shares, shares_low),
    )


def backward_window(saved, grads, latent_query):
    weights, mixed, shares, shares_low = saved
    width = latent_query.shape[1]
    head_size = width // HEADS
    groups = grads.shape[0]
    count_latent = latent_query.shape[0]
    scale = 1.0 / math.sqrt(head_size)
    grad_blocks = grads.reshape(groups, count_latent, HEADS, head_size)
    share_grads = jnp.einsum(
        "glhd,grhd->ghlr", grad_blocks, mixed, preferred_element_type=jnp.float32
    )
    centre = jnp.sum(shares * share_grads, axis=-1, keepdims=True)
    score_grads = shares * (share_grads - centre) * scale
    from_values = jnp.einsum(
        "ghlr,glhd->grhd", shares_low, grad_blocks, preferred_element_type=jnp.float32
    )
    query_wide = latent_query.reshape(count_latent, HEADS, head_size).astype(jnp.float32)
    from_keys = jnp.einsum(
        "ghlr,lhd->grhd", score_grads, query_wide, precision=lax.Precision.HIGHEST
    )
    mixed_grad = (from_values + from_keys).astype(jnp.bfloat16)
    value_grad = jnp.einsum(
        "ghqc,gqhd->gchd", weights, mixed_grad, preferred_element_type=jnp.float32
    ).astype(jnp.bfloat16)
    return value_grad.reshape(groups * value_grad.shape[1], width)


def copies(piece, count):
    return jnp.broadcast_to(piece[None], (count,) + piece.shape)


def exchange(array, axes):
    return lax.all_to_all(array, axes, 0, 0, tiled=True)


def own_half(array, index, axis):
    low, high = jnp.split(array, 2, axis=axis)
    return jnp.where(index == 0, low, high), jnp.where(index == 0, high, low)


def on_device(patches, counts, norm_gain, norm_bias, input_weight, latent_query, cotangent):
    slots, capacity, width_in = patches.shape[2:]
    latent_count, width = cotangent.shape[3:]
    depth = input_weight.shape[0]
    ring = lax.axis_size("z")
    sharers = lax.axis_size(PLANE)
    xp, xi, y, c = (lax.axis_index(a) for a in DP)
    pair = 2 * xi + c
    quarter = width // 4

    images = patches.reshape(slots * capacity, width_in)
    grads = cotangent.reshape(slots * latent_count, width)
    sizes = jnp.zeros((16, width), jnp.bfloat16) + jnp.pad(
        counts.reshape(slots).astype(jnp.bfloat16), (0, 16 - slots)
    )[:, None]
    ride = jnp.concatenate([grads, sizes], axis=0)

    keep, give = own_half(ride, xi, 1)
    images_x = lax.ppermute(images, "xi", SWAP)
    ride_x = lax.ppermute(give, "xi", SWAP)

    piece = quarter // 4
    rows = lax.dynamic_slice_in_dim(input_weight, xp * (depth // 2), depth // 2, 0)
    target = jnp.arange(3 * piece, dtype=jnp.int32)
    source = width * (target // piece) + quarter * pair + piece * y + target % piece
    pick = (jnp.arange(3 * width, dtype=jnp.int32)[:, None] == source[None, :]).astype(jnp.bfloat16)
    own = jnp.dot(rows, pick, preferred_element_type=jnp.float32).astype(jnp.bfloat16)
    along = exchange(copies(own, ring), "z")

    images_two = jnp.stack([images, images_x])
    mine, theirs = own_half(jnp.stack([keep, ride_x]), c, 2)
    images_c = lax.ppermute(images_two, "c", SWAP)
    ride_c = lax.ppermute(theirs, "c", SWAP)

    whole = exchange(copies(along, sharers), PLANE)
    weight = (
        whole.reshape(2, 4, ring, depth // 2, 3, piece)
        .transpose(2, 0, 3, 4, 1, 5)
        .reshape(ring * depth, 3 * quarter)
    )

    rides = jnp.concatenate([mine, ride_c])
    sizes_all = rides[:, slots * latent_count :][:, :slots, 0].astype(jnp.int32).reshape(4 * slots)
    grads_all = rides[:, : slots * latent_count].reshape(4 * slots, latent_count, quarter)
    normed = layer_norm(jnp.concatenate([images_two, images_c]), norm_gain, norm_bias)
    normed = normed.reshape(4 * slots * capacity, width_in)
    projected = jnp.dot(normed, weight, preferred_element_type=jnp.float32)
    query = lax.dynamic_slice_in_dim(latent_query, pair * quarter, quarter, 1)
    latents, saved = forward_window(projected, sizes_all, query)
    value_grad = backward_window(saved, grads_all, query)
    partial = jnp.einsum("rd,rv->dv", normed, value_grad, preferred_element_type=jnp.float32)

    part = depth // sharers
    partial = partial.astype(jnp.bfloat16).reshape(ring, sharers, part, quarter)
    came = exchange(partial.transpose(1, 0, 2, 3), PLANE)
    summed = jnp.sum(came.astype(jnp.float32), axis=0)
    summed = jnp.sum(exchange(summed, "z"), axis=0)
    done = exchange(copies(summed, 4 * sharers), DP)
    grad_value = (
        done.reshape(2, 2, 4, 2, part, quarter).transpose(0, 2, 4, 1, 3, 5).reshape(depth, width)
    )

    latents = latents.reshape(2, 2, slots, latent_count, quarter)
    other_c = lax.ppermute(latents[1], "c", SWAP)
    by_c = jnp.where(c == 0, jnp.stack([latents[0], other_c]), jnp.stack([other_c, latents[0]]))
    other_x = lax.ppermute(by_c[:, 1], "xi", SWAP)
    own_x = by_c[:, 0]
    by_x = jnp.where(xi == 0, jnp.stack([own_x, other_x]), jnp.stack([other_x, own_x]))
    latents_own = by_x.transpose(2, 3, 0, 1, 4).reshape(cotangent.shape)
    return latents_own, grad_value


def solution(mesh):
    fine = Mesh(mesh.devices.reshape(2, 2, 4, 2, 16), DP + ("z",))
    placed = (
        P(DP, "z", None, None, None),
        P(DP, "z", None),
        P(),
        P(),
        P("z", None),
        P(),
        P(DP, "z", None, None, None),
    )
    return jax.shard_map(
        on_device,
        mesh=fine,
        in_specs=placed,
        out_specs=(P(DP, "z", None, None, None), P("z", None)),
        check_vma=False,
    )
```

```python
import functools
import math

import jax
import jax.numpy as jnp
from jax import lax
from jax.experimental import pallas as pl
from jax.experimental.pallas import tpu as pltpu
from jax.sharding import Mesh
from jax.sharding import PartitionSpec as P

HEADS = 2
EPSILON = 1e-06
MASKED = -1e30
DP = ("xp", "xi", "y", "c")
PLANE = ("xp", "y")
SWAP = [(0, 1), (1, 0)]
LANES = 128
CHUNK = 16
LIMIT = 56 * 1024 * 1024


def norm_kernel(first_ref, second_ref, gain_ref, bias_ref, out_ref):
    gain, bias = gain_ref[...], bias_ref[...]
    for index, source in enumerate((first_ref, second_ref)):
        for start in range(0, source.shape[0], CHUNK):
            values = source[start : start + CHUNK, :].astype(jnp.float32)
            centre = values - jnp.mean(values, axis=-1, keepdims=True)
            spread = jnp.mean(centre * centre, axis=-1, keepdims=True)
            normed = centre * lax.rsqrt(spread + EPSILON) * gain + bias
            out_ref[index, start : start + CHUNK, :] = normed.astype(jnp.bfloat16)


def across(left, right):
    return lax.dot_general(left, right, (((1,), (1,)), ((), ())), preferred_element_type=jnp.float32)


def along(left, right):
    return lax.dot_general(left, right, (((0,), (0,)), ((), ())), preferred_element_type=jnp.float32)


def plain(left, right):
    return jnp.dot(left, right, preferred_element_type=jnp.float32)


def column_order(piece, quarter):
    out = lax.broadcasted_iota(jnp.int32, (4 * LANES, 6 * LANES), 1)
    row = lax.broadcasted_iota(jnp.int32, (4 * LANES, 6 * LANES), 0)
    kind = (out >= 2 * LANES).astype(jnp.int32) + (out >= 4 * LANES).astype(jnp.int32)
    lane = out - 2 * LANES * kind
    block = sum((lane >= piece * n).astype(jnp.int32) for n in (1, 2, 3))
    source = LANES * block + piece * kind + lane - piece * block
    return jnp.where((row == source) & (lane < quarter), 1.0, 0.0).astype(jnp.bfloat16)


def main_kernel(
    slots, latent_count, ring, sharers,
    here_ref, there_ref, whole_ref, ride_ref, ride_c_ref, query_ref,
    lat_ref, lat_c_ref, packed_ref,
    weight_ref, grad_ref, total_ref, tail_ref,
):
    rows, width_in = here_ref.shape[1:]
    capacity = rows // slots
    quarter = query_ref.shape[1]
    head_size = quarter // HEADS
    piece = quarter // 4
    scale = 1.0 / math.sqrt(head_size)
    for block in range(4):
        halves = [whole_ref[4 * half + block].astype(jnp.float32) for half in range(2)]
        stacked = jnp.stack(halves, axis=1).reshape(width_in, LANES)
        weight_ref[:, LANES * block : LANES * (block + 1)] = stacked.astype(jnp.bfloat16)
    order = column_order(piece, quarter)
    first_head = lax.broadcasted_iota(jnp.int32, (1, quarter), 1) < head_size
    nothing = jnp.zeros((), jnp.bfloat16)

    def head_of(array, head):
        return jnp.where(first_head, array, nothing) if head == 0 else jnp.where(first_head, nothing, array)

    def both_heads(array):
        return jnp.concatenate([head_of(array, 0), head_of(array, 1)], axis=0)

    query_wide = both_heads(query_ref[...])
    grad_ref[...] = jnp.zeros_like(grad_ref)
    image_of = [
        sum((lax.broadcasted_iota(jnp.int32, shape, axis) >= capacity * n).astype(jnp.int32) for n in range(1, slots))
        for shape, axis in (((rows, 1), 0), ((1, rows), 1))
    ]
    place = [
        (lax.broadcasted_iota(jnp.int32, shape, axis) - capacity * image).astype(jnp.float32)
        for (shape, axis), image in zip((((rows, 1), 0), ((1, rows), 1)), image_of)
    ]
    offset = lax.broadcasted_iota(jnp.int32, (capacity, 1), 0).astype(jnp.float32)
    for block in range(4):
        normed_ref, carried_ref, out_ref = (
            (here_ref, ride_ref, lat_ref) if block < 2 else (there_ref, ride_c_ref, lat_c_ref)
        )
        side = block % 2
        sizes = carried_ref[side, slots * latent_count :, :].astype(jnp.float32)
        size = [sizes[n : n + 1, 0:1] for n in range(slots)]
        live = []
        for image, position in zip(image_of, place):
            limit = size[slots - 1] + jnp.zeros_like(position)
            for n in reversed(range(slots - 1)):
                limit = jnp.where(image == n, size[n], limit)
            live.append(position < limit)
        row_label = jnp.where(live[0], image_of[0], -1)
        column_label = jnp.where(live[1], image_of[1], -2)
        allowed = row_label == column_label
        projected = plain(normed_ref[side], weight_ref[...]).astype(jnp.bfloat16)
        sorted_columns = plain(projected, order).astype(jnp.bfloat16)
        queries, keys, values = (
            sorted_columns[:, 2 * LANES * n : 2 * LANES * n + quarter] for n in range(3)
        )
        weights = []
        for head in range(HEADS):
            scores = jnp.where(allowed, across(head_of(queries, head), keys) * scale, MASKED)
            highest = jnp.max(scores, axis=-1, keepdims=True)
            raised = jnp.where(allowed, jnp.exp(scores - highest), 0.0)
            total = jnp.maximum(jnp.sum(raised, axis=-1, keepdims=True), 1.0)
            weights.append((raised / total).astype(jnp.bfloat16))
        mixed = sum(plain(weights[head], head_of(values, head)) for head in range(HEADS))
        mixed = mixed.astype(jnp.bfloat16)
        latent_scores = across(mixed, query_wide) * scale
        mixed_grads = []
        for n in range(slots):
            span = slice(capacity * n, capacity * (n + 1))
            inside = offset < size[n]
            masked = jnp.where(inside, latent_scores[span], MASKED)
            raised = jnp.where(inside, jnp.exp(masked - jnp.max(masked, axis=0, keepdims=True)), 0.0)
            shares = raised / jnp.maximum(jnp.sum(raised, axis=0, keepdims=True), 1.0)
            shares_low = shares.astype(jnp.bfloat16)
            mixed_here = mixed[span]
            latents = along(shares_low, mixed_here)
            out_ref[side, latent_count * n : latent_count * (n + 1), :] = jnp.where(
                first_head, latents[:latent_count], latents[latent_count:]
            )
            cotangent = both_heads(carried_ref[side, latent_count * n : latent_count * (n + 1), :])
            share_grads = across(mixed_here, cotangent)
            middle = jnp.sum(shares * share_grads, axis=0, keepdims=True)
            score_grads = shares * (share_grads - middle) * scale
            high = score_grads.astype(jnp.bfloat16)
            low = (score_grads - high.astype(jnp.float32)).astype(jnp.bfloat16)
            mixed_grad = plain(shares_low, cotangent) + (plain(high, query_wide) + plain(low, query_wide))
            mixed_grads.append(mixed_grad.astype(jnp.bfloat16))
        mixed_grad = jnp.concatenate(mixed_grads, axis=0)
        value_grad = sum(along(weights[head], head_of(mixed_grad, head)) for head in range(HEADS))
        grad_ref[rows * block : rows * (block + 1), :quarter] = value_grad.astype(jnp.bfloat16)
    total = sum(
        along(ref[side], grad_ref[rows * (2 * n + side) : rows * (2 * n + side + 1), :])
        for n, ref in enumerate((here_ref, there_ref))
        for side in range(2)
    )
    total_ref[...] = total[:, :LANES]
    tail_ref[...] = total[:, LANES:]
    depth = width_in // ring
    part = depth // sharers
    per_tile = 2 * LANES // (2 * (quarter - LANES))
    for sharer in range(sharers):
        rest = []
        for row in range(part):
            picked = pl.ds(sharer * part + row, ring, stride=depth)
            packed_ref[sharer, :, LANES * row : LANES * (row + 1)] = total_ref[picked, :].astype(jnp.bfloat16)
            tail = tail_ref[picked, :]
            shift = (row % per_tile) * (quarter - LANES)
            tail = tail if shift == 0 else pltpu.roll(tail, shift, 1)
            if shift == 0:
                rest.append(tail)
            else:
                rest[-1] = rest[-1] + tail
        for n, tile in enumerate(rest):
            lanes = slice(LANES * (part + n), LANES * (part + n + 1))
            packed_ref[sharer, :, lanes] = tile.astype(jnp.bfloat16)


def call(kernel, outs, scratch, flops, *operands):
    memory = pl.BlockSpec(memory_space=pltpu.VMEM)
    size = sum(math.prod(a.shape) * a.dtype.itemsize for a in (*operands, *outs))
    return pl.pallas_call(
        kernel,
        out_shape=outs,
        in_specs=[memory] * len(operands),
        out_specs=[memory] * len(outs),
        scratch_shapes=scratch,
        compiler_params=pltpu.CompilerParams(vmem_limit_bytes=LIMIT),
        cost_estimate=pl.CostEstimate(flops=flops, bytes_accessed=size, transcendentals=0),
    )(*operands)


def layer_norm(first, second, gain, bias):
    out = jax.ShapeDtypeStruct((2,) + first.shape, jnp.bfloat16)
    return call(norm_kernel, [out], [], 20 * 2 * first.size, first, second, gain[None], bias[None])[0]


def attend(here, there, whole, ride, ride_c, query, slots, latent_count, ring):
    rows, width_in = here.shape[1:]
    quarter = query.shape[1]
    sharers = whole.shape[0]
    part = width_in // ring // sharers
    packed = LANES * (part + -(-part * (quarter - LANES) // LANES))
    latents = jax.ShapeDtypeStruct((2, slots * latent_count, quarter), jnp.float32)
    return call(
        functools.partial(main_kernel, slots, latent_count, ring, sharers),
        [latents, latents, jax.ShapeDtypeStruct((sharers, ring, packed), jnp.bfloat16)],
        [
            pltpu.VMEM((width_in, 4 * LANES), jnp.bfloat16),
            pltpu.VMEM((4 * rows, 2 * LANES), jnp.bfloat16),
            pltpu.VMEM((width_in, LANES), jnp.float32),
            pltpu.VMEM((width_in, LANES), jnp.float32),
        ],
        2 * 4 * rows * width_in * 5 * quarter,
        here, there, whole, ride, ride_c, query,
    )


def copies(piece, count):
    return jnp.broadcast_to(piece[None], (count,) + piece.shape)


def exchange(array, axes):
    return lax.all_to_all(array, axes, 0, 0, tiled=True)


def own_half(array, index, axis):
    low, high = jnp.split(array, 2, axis=axis)
    return jnp.where(index == 0, low, high), jnp.where(index == 0, high, low)


def in_order(own, other, index):
    return jnp.where(
        index == 0, jnp.concatenate([own, other], axis=-1), jnp.concatenate([other, own], axis=-1)
    )


def unpack(packed, part, quarter):
    lead = packed.shape[:-1]
    head = packed[..., : LANES * part].reshape(lead + (part, LANES))
    rest = packed[..., LANES * part : LANES * part + part * (quarter - LANES)]
    return jnp.concatenate([head, rest.reshape(lead + (part, quarter - LANES))], axis=-1)


def on_device(patches, counts, norm_gain, norm_bias, input_weight, latent_query, cotangent):
    slots, capacity, width_in = patches.shape[2:]
    latent_count, width = cotangent.shape[3:]
    depth = input_weight.shape[0]
    ring = lax.axis_size("z")
    sharers = lax.axis_size(PLANE)
    xp, xi, y, c = (lax.axis_index(a) for a in DP)
    pair = 2 * xi + c
    quarter = width // 4

    images = patches.reshape(slots * capacity, width_in)
    grads = cotangent.reshape(slots * latent_count, width)
    sizes = jnp.zeros((16, width), jnp.bfloat16) + jnp.pad(
        counts.reshape(slots).astype(jnp.bfloat16), (0, 16 - slots)
    )[:, None]
    ride = jnp.concatenate([grads, sizes], axis=0)

    keep, give = own_half(ride, xi, 1)
    images_x = lax.ppermute(images, "xi", SWAP)
    ride_x = lax.ppermute(give, "xi", SWAP)

    piece = quarter // 4
    rows = lax.dynamic_slice_in_dim(input_weight, xp * (depth // 2), depth // 2, 0)
    target = jnp.arange(LANES, dtype=jnp.int32)
    source = width * (target // piece) + quarter * pair + piece * y + target % piece
    source = jnp.where(target < 3 * piece, source, -1)
    pick = (jnp.arange(3 * width, dtype=jnp.int32)[:, None] == source[None, :]).astype(jnp.bfloat16)
    own = jnp.dot(rows, pick, preferred_element_type=jnp.float32).astype(jnp.bfloat16)
    gathered = exchange(copies(own, ring), "z")

    normed = layer_norm(images, images_x, norm_gain, norm_bias)
    mine, theirs = own_half(jnp.stack([keep, ride_x]), c, 2)
    normed_c = lax.ppermute(normed, "c", SWAP)
    ride_c = lax.ppermute(theirs, "c", SWAP)

    whole = exchange(copies(gathered, sharers), PLANE)
    query = lax.dynamic_slice_in_dim(latent_query, pair * quarter, quarter, 1)
    latents, latents_c, packed = attend(
        normed, normed_c, whole, mine, ride_c, query, slots, latent_count, ring
    )

    part = depth // sharers
    summed = jnp.sum(exchange(packed, PLANE).astype(jnp.float32), axis=0)
    summed = jnp.sum(exchange(summed, "z"), axis=0)
    done = unpack(exchange(copies(summed, 4 * sharers), DP), part, quarter)
    grad_value = (
        done.reshape(2, 2, 4, 2, part, quarter).transpose(0, 2, 4, 1, 3, 5).reshape(depth, width)
    )

    latents_c = lax.ppermute(latents_c, "c", SWAP)
    by_c = in_order(latents, latents_c, c)
    by_x = in_order(by_c[0], lax.ppermute(by_c[1], "xi", SWAP), xi)
    return by_x.reshape(cotangent.shape), grad_value


def solution(mesh):
    fine = Mesh(mesh.devices.reshape(2, 2, 4, 2, 16), DP + ("z",))
    placed = (
        P(DP, "z", None, None, None),
        P(DP, "z", None),
        P(),
        P(),
        P("z", None),
        P(),
        P(DP, "z", None, None, None),
    )
    return jax.shard_map(
        on_device,
        mesh=fine,
        in_specs=placed,
        out_specs=(P(DP, "z", None, None, None), P("z", None)),
        check_vma=False,
    )
```

```python
import functools
import math

import jax
import jax.numpy as jnp
from jax import lax
from jax.experimental import pallas as pl
from jax.experimental.pallas import tpu as pltpu
from jax.sharding import Mesh
from jax.sharding import PartitionSpec as P

HEADS = 2
EPSILON = 1e-06
MASKED = -1e30
DP = ("xp", "xi", "y", "c")
PLANE = ("xp", "y")
SWAP = [(0, 1), (1, 0)]
LANES = 128
CHUNK = 16
WAVE = 4
LIMIT = 56 * 1024 * 1024


def pack_kernel(place_ref, counts_ref, images_ref, grads_ref, send_ref, keep_ref):
    rows, half = images_ref.shape[0], grads_ref.shape[1] // 2
    slots = counts_ref.shape[0]
    latent_count = grads_ref.shape[0] // slots
    row = iota((latent_count, half), 0)
    counts = jnp.zeros((latent_count, half), jnp.float32)
    for n in range(slots):
        counts = jnp.where(row == n, counts_ref[n].astype(jnp.float32), counts)
    blocks = [grads_ref[latent_count * n : latent_count * (n + 1), :] for n in range(slots)]
    low = jnp.concatenate([block[:, :half] for block in blocks] + [counts.astype(jnp.bfloat16)], axis=1)
    high = jnp.concatenate([block[:, half:] for block in blocks] + [counts.astype(jnp.bfloat16)], axis=1)
    first = place_ref[0] == 0
    send_ref[:rows, :] = images_ref[...]
    send_ref[rows:, :] = jnp.where(first, high, low)
    keep_ref[...] = jnp.where(first, low, high)


def norm_kernel(images_ref, keep_ref, came_ref, gain_ref, bias_ref, out_ref):
    gain, bias = gain_ref[...].reshape(1, -1), bias_ref[...].reshape(1, -1)
    rows = images_ref.shape[0]
    for index, source in enumerate((images_ref, came_ref)):
        for start in range(0, rows, CHUNK):
            values = source[start : start + CHUNK, :].astype(jnp.float32)
            centre = values - jnp.mean(values, axis=-1, keepdims=True)
            spread = jnp.mean(centre * centre, axis=-1, keepdims=True)
            normed = centre * lax.rsqrt(spread + EPSILON) * gain + bias
            out_ref[index, start : start + CHUNK, :] = normed.astype(jnp.bfloat16)
    out_ref[0, rows:, :] = keep_ref[...]
    out_ref[1, rows:, :] = came_ref[rows:, :]


def across(left, right):
    return lax.dot_general(left, right, (((1,), (1,)), ((), ())), preferred_element_type=jnp.float32)


def along(left, right):
    return lax.dot_general(left, right, (((0,), (0,)), ((), ())), preferred_element_type=jnp.float32)


def plain(left, right):
    return jnp.dot(left, right, preferred_element_type=jnp.float32)


def one_hot(chosen):
    return jnp.where(chosen, 1.0, 0.0).astype(jnp.bfloat16)


def iota(shape, axis):
    return lax.broadcasted_iota(jnp.int32, shape, axis)


def column_order(piece, quarter):
    row, out = iota((4 * LANES, 6 * LANES), 0), iota((4 * LANES, 6 * LANES), 1)
    kind = (out >= 2 * LANES).astype(jnp.int32) + (out >= 4 * LANES).astype(jnp.int32)
    lane = out - 2 * LANES * kind
    block = sum((lane >= piece * n).astype(jnp.int32) for n in (1, 2, 3))
    source = LANES * block + piece * kind + lane - piece * block
    return one_hot((row == source) & (lane < quarter))


def main_kernel(
    slots, latent_count, ring, sharers,
    index_ref, near_ref, far_ref, whole_ref, query_ref,
    lat_ref, lat_c_ref, packed_ref,
    weight_ref, grad_ref, total_ref, tail_ref,
):
    width_in = near_ref.shape[2]
    rows = near_ref.shape[1] - latent_count
    capacity = rows // slots
    quarter = lat_ref.shape[2]
    head_size = quarter // HEADS
    scale = 1.0 / math.sqrt(head_size)
    for block in range(4):
        halves = [whole_ref[4 * half + block].astype(jnp.float32) for half in range(2)]
        stacked = jnp.stack(halves, axis=1).reshape(width_in, LANES)
        weight_ref[:, LANES * block : LANES * (block + 1)] = stacked.astype(jnp.bfloat16)
    order = column_order(quarter // 4, quarter)
    first_head = iota((1, quarter), 1) < head_size
    nothing = jnp.zeros((), jnp.bfloat16)

    def head_of(array, head):
        return jnp.where(first_head, array, nothing) if head == 0 else jnp.where(first_head, nothing, array)

    def both_heads(array):
        return jnp.concatenate([head_of(array, 0), head_of(array, 1)], axis=0)

    width = query_ref.shape[1]
    pick = one_hot(
        (iota((width, 2 * LANES), 0) == quarter * index_ref[0] + iota((width, 2 * LANES), 1))
        & (iota((width, 2 * LANES), 1) < quarter)
    )
    query = both_heads(plain(query_ref[...], pick).astype(jnp.bfloat16)[:, :quarter])
    grad_ref[...] = jnp.zeros_like(grad_ref)
    image_of = [
        sum((iota(shape, axis) >= capacity * n).astype(jnp.int32) for n in range(1, slots))
        for shape, axis in (((rows, 1), 0), ((1, rows), 1))
    ]
    place = [
        (iota(shape, axis) - capacity * image).astype(jnp.float32)
        for (shape, axis), image in zip((((rows, 1), 0), ((1, rows), 1)), image_of)
    ]
    members = [ref.at[n] for ref in (near_ref, far_ref) for n in range(ref.shape[0])]
    first_pair = index_ref[0] % 2 == 0
    outs = [ref.at[n] for ref in (lat_ref, lat_c_ref) for n in range(ref.shape[0])]
    apart = slots, capacity, HEADS * latent_count

    def limits(block):
        sizes = members[block][rows : rows + 16, 2 * quarter * slots :].astype(jnp.float32)
        size = [sizes[n : n + 1, 0:1] for n in range(slots)]
        live = []
        for image, position in zip(image_of, place):
            limit = size[slots - 1] + jnp.zeros_like(position)
            for n in reversed(range(slots - 1)):
                limit = jnp.where(image == n, size[n], limit)
            live.append(position < limit)
        return jnp.where(live[0], image_of[0], -1), jnp.where(live[1], image_of[1], -2)

    def attention(scores, allowed):
        scores = jnp.where(allowed, scores * scale, MASKED)
        highest = jnp.max(scores, axis=-1, keepdims=True)
        raised = jnp.where(allowed, jnp.exp(scores - highest), 0.0)
        total = jnp.maximum(jnp.sum(raised, axis=-1, keepdims=True), 1.0)
        return (raised * (1.0 / total)).astype(jnp.bfloat16)

    def over_patches(scores, labels):
        inside = (labels[0] >= 0).reshape(slots, capacity, 1)
        masked = jnp.where(inside, scores.reshape(apart) * scale, MASKED)
        raised = jnp.where(inside, jnp.exp(masked - jnp.max(masked, axis=1, keepdims=True)), 0.0)
        return raised * (1.0 / jnp.maximum(jnp.sum(raised, axis=1, keepdims=True), 1.0))

    def normed(block):
        return members[block][:rows, :]

    def cotangent_of(block, n):
        ride = members[block][rows:, 2 * quarter * n : 2 * quarter * (n + 1)]
        return both_heads(jnp.where(first_pair, ride[:, :quarter], ride[:, quarter:]))

    def span(n):
        return slice(latent_count * n, latent_count * (n + 1))

    for first in range(0, len(members), WAVE):
        blocks = range(first, min(first + WAVE, len(members)))
        labels = [limits(b) for b in blocks]
        projected = [plain(normed(b), weight_ref[...]).astype(jnp.bfloat16) for b in blocks]
        parts = [plain(p, order).astype(jnp.bfloat16) for p in projected]
        parts = [[p[:, 2 * LANES * n : 2 * LANES * n + quarter] for n in range(3)] for p in parts]
        scores = [[across(head_of(q, h), k) for h in range(HEADS)] for q, k, _ in parts]
        weights = [[attention(s, m[0] == m[1]) for s in both] for both, m in zip(scores, labels)]
        mixed = [
            sum(plain(w[h], head_of(v, h)) for h in range(HEADS)).astype(jnp.bfloat16)
            for w, (_, _, v) in zip(weights, parts)
        ]
        shares = [over_patches(across(m, query), l) for m, l in zip(mixed, labels)]
        low = [s.astype(jnp.bfloat16) for s in shares]
        split = [m.reshape(slots, capacity, quarter) for m in mixed]
        cotangent = [[cotangent_of(b, n) for n in range(slots)] for b in blocks]
        share_grads = [
            jnp.stack([across(s[n], g[n]) for n in range(slots)]) for s, g in zip(split, cotangent)
        ]
        for b, l, s in zip(blocks, low, split):
            for n in range(slots):
                latents = along(l[n], s[n])
                outs[b][span(n), :] = jnp.where(first_head, latents[:latent_count], latents[latent_count:])
        score_grads = [
            s * (g - jnp.sum(s * g, axis=1, keepdims=True)) * scale for s, g in zip(shares, share_grads)
        ]
        score_grads = [g.reshape(rows, HEADS * latent_count) for g in score_grads]
        high = [g.astype(jnp.bfloat16) for g in score_grads]
        rest = [(g - h.astype(jnp.float32)).astype(jnp.bfloat16) for g, h in zip(score_grads, high)]
        from_values = [
            jnp.concatenate([plain(l[n], g[n]) for n in range(slots)], axis=0) for l, g in zip(low, cotangent)
        ]
        mixed_grad = [
            (v + (plain(h, query) + plain(r, query))).astype(jnp.bfloat16)
            for v, h, r in zip(from_values, high, rest)
        ]
        for b, w, g in zip(blocks, weights, mixed_grad):
            value_grad = sum(along(w[h], head_of(g, h)) for h in range(HEADS))
            grad_ref[rows * b : rows * (b + 1), :quarter] = value_grad.astype(jnp.bfloat16)
    total = sum(
        along(grad_ref[rows * b : rows * (b + 1), :], normed(b)) for b in range(len(members))
    )
    total_ref[...] = total[:LANES].T
    tail_ref[...] = total[LANES:].T
    depth = width_in // ring
    part = depth // sharers
    per_tile = LANES // (quarter - LANES)
    for sharer in range(sharers):
        rest = []
        for row in range(part):
            picked = pl.ds(sharer * part + row, ring, stride=depth)
            packed_ref[sharer, :, LANES * row : LANES * (row + 1)] = total_ref[picked, :].astype(jnp.bfloat16)
            tail = tail_ref[picked, :]
            shift = (row % per_tile) * (quarter - LANES)
            if shift == 0:
                rest.append(tail)
            else:
                rest[-1] = rest[-1] + pltpu.roll(tail, shift, 1)
        for n, tile in enumerate(rest):
            lanes = slice(LANES * (part + n), LANES * (part + n + 1))
            packed_ref[sharer, :, lanes] = tile.astype(jnp.bfloat16)


def order_kernel(index_ref, own_ref, x_ref, out_ref, parts_ref):
    quarter = own_ref.shape[2]
    parts_ref[:2] = own_ref[...]
    parts_ref[2:] = x_ref[...]
    for pair in range(4):
        out_ref[:, quarter * pair : quarter * (pair + 1)] = parts_ref[pair ^ index_ref[0]]


def call(kernel, outs, scratch, flops, *operands):
    memory = pl.BlockSpec(memory_space=pltpu.VMEM)
    scalars = pl.BlockSpec(memory_space=pltpu.SMEM)
    size = sum(math.prod(a.shape) * a.dtype.itemsize for a in (*operands, *outs))
    return pl.pallas_call(
        kernel,
        out_shape=outs,
        in_specs=[scalars if a.dtype == jnp.int32 else memory for a in operands],
        out_specs=[memory] * len(outs),
        scratch_shapes=scratch,
        compiler_params=pltpu.CompilerParams(vmem_limit_bytes=LIMIT),
        cost_estimate=pl.CostEstimate(flops=flops, bytes_accessed=size, transcendentals=0),
    )(*operands)


def pack(place, counts, images, grads):
    below = grads.shape[0] // counts.shape[0]
    send = jax.ShapeDtypeStruct((images.shape[0] + below, images.shape[1]), jnp.bfloat16)
    keep = jax.ShapeDtypeStruct((below, images.shape[1]), jnp.bfloat16)
    return call(pack_kernel, [send, keep], [], images.size, place, counts, images, grads)


def layer_norm(images, keep, came, gain, bias):
    out = jax.ShapeDtypeStruct((2,) + came.shape, jnp.bfloat16)
    return call(norm_kernel, [out], [], 40 * images.size, images, keep, came, gain, bias)[0]


def attend(index, near, far, whole, query, slots, latent_count, ring):
    width_in = near.shape[2]
    rows = near.shape[1] - latent_count
    quarter = query.shape[1] // 4
    sharers = whole.shape[0]
    part = width_in // ring // sharers
    packed = LANES * (part + -(-part * (quarter - LANES) // LANES))
    latents = jax.ShapeDtypeStruct((2, slots * latent_count, quarter), jnp.float32)
    return call(
        functools.partial(main_kernel, slots, latent_count, ring, sharers),
        [latents, latents, jax.ShapeDtypeStruct((sharers, ring, packed), jnp.bfloat16)],
        [
            pltpu.VMEM((width_in, 4 * LANES), jnp.bfloat16),
            pltpu.VMEM((4 * rows, 2 * LANES), jnp.bfloat16),
            pltpu.VMEM((width_in, LANES), jnp.float32),
            pltpu.VMEM((width_in, LANES), jnp.float32),
        ],
        2 * 4 * rows * width_in * 5 * quarter,
        index, near, far, whole, query,
    )


def copies(piece, count):
    return jnp.broadcast_to(piece[None], (count,) + piece.shape)


def exchange(array, axes):
    return lax.all_to_all(array, axes, 0, 0, tiled=True)


def unpack(packed, part, quarter):
    lead = packed.shape[:-1]
    head = packed[..., : LANES * part].reshape(lead + (part, LANES))
    rest = packed[..., LANES * part : LANES * part + part * (quarter - LANES)]
    return jnp.concatenate([head, rest.reshape(lead + (part, quarter - LANES))], axis=-1)


def on_device(patches, counts, norm_gain, norm_bias, input_weight, latent_query, cotangent):
    slots, capacity, width_in = patches.shape[2:]
    latent_count, width = cotangent.shape[3:]
    depth = input_weight.shape[0]
    ring = lax.axis_size("z")
    sharers = lax.axis_size(PLANE)
    xp, xi, y, c = (lax.axis_index(a) for a in DP)
    pair = 2 * xi + c
    quarter = width // 4

    images = patches.reshape(slots * capacity, width_in)
    grads = cotangent.reshape(slots * latent_count, width)
    send, keep = pack(xi.astype(jnp.int32).reshape(1), counts.reshape(slots), images, grads)
    came = lax.ppermute(send, "xi", SWAP)

    piece = quarter // 4
    rows = lax.dynamic_slice_in_dim(input_weight, xp * (depth // 2), depth // 2, 0)
    target = jnp.arange(LANES, dtype=jnp.int32)
    source = width * (target // piece) + quarter * pair + piece * y + target % piece
    source = jnp.where(target < 3 * piece, source, -1)
    pick = (jnp.arange(3 * width, dtype=jnp.int32)[:, None] == source[None, :]).astype(jnp.bfloat16)
    own = jnp.dot(rows, pick, preferred_element_type=jnp.float32).astype(jnp.bfloat16)
    gathered = exchange(copies(own, ring), "z")

    normed = layer_norm(images, keep, came, norm_gain, norm_bias)
    gathered, normed = lax.optimization_barrier((gathered, normed))
    normed_c = lax.ppermute(normed, "c", SWAP)

    whole = exchange(copies(gathered, sharers), PLANE)
    index = pair.astype(jnp.int32).reshape(1)
    latents, latents_c, packed = attend(
        index, normed, normed_c, whole, latent_query, slots, latent_count, ring
    )

    part = depth // sharers
    summed = jnp.sum(exchange(packed, PLANE).astype(jnp.float32), axis=0)
    summed, latents_c = lax.optimization_barrier((summed, latents_c))
    both = jnp.stack([latents, lax.ppermute(latents_c, "c", SWAP)], axis=1)
    summed = jnp.sum(exchange(summed, "z"), axis=0)
    latents_x = lax.ppermute(both[1], "xi", SWAP)
    done = unpack(exchange(copies(summed, 4 * sharers), DP), part, quarter)
    grad_value = (
        done.reshape(2, 2, 4, 2, part, quarter).transpose(0, 2, 4, 1, 3, 5).reshape(depth, width)
    )

    shape = jax.ShapeDtypeStruct((slots * latent_count, width), jnp.float32)
    parts = pltpu.VMEM((4,) + latents.shape[1:], jnp.float32)
    latents = call(order_kernel, [shape], [parts], both.size, index, both[0], latents_x)[0]
    return latents.reshape(cotangent.shape), grad_value


def solution(mesh):
    fine = Mesh(mesh.devices.reshape(2, 2, 4, 2, 16), DP + ("z",))
    placed = (
        P(DP, "z", None, None, None),
        P(DP, "z", None),
        P(),
        P(),
        P("z", None),
        P(),
        P(DP, "z", None, None, None),
    )
    return jax.shard_map(
        on_device,
        mesh=fine,
        in_specs=placed,
        out_specs=(P(DP, "z", None, None, None), P("z", None)),
        check_vma=False,
    )
```

```python
import functools
import math

import jax
import jax.numpy as jnp
from jax import lax
from jax.experimental import pallas as pl
from jax.experimental.pallas import tpu as pltpu
from jax.sharding import Mesh
from jax.sharding import PartitionSpec as P

HEADS = 2
EPSILON = 1e-06
MASKED = -1e30
DP = ("xp", "xi", "y", "c")
PLANE = ("xp", "y")
SWAP = [(0, 1), (1, 0)]
LANES = 128
CHUNK = 16
WAVE = 4
MIB = 1024 * 1024


def pack_kernel(place_ref, counts_ref, images_ref, grads_ref, send_ref, keep_ref):
    rows, half = images_ref.shape[0], grads_ref.shape[1] // 2
    slots = counts_ref.shape[0]
    latent_count = grads_ref.shape[0] // slots
    row = iota((latent_count, half), 0)
    counts = jnp.zeros((latent_count, half), jnp.float32)
    for n in range(slots):
        counts = jnp.where(row == n, counts_ref[n].astype(jnp.float32), counts)
    blocks = [grads_ref[latent_count * n : latent_count * (n + 1), :] for n in range(slots)]
    low = jnp.concatenate([block[:, :half] for block in blocks] + [counts.astype(jnp.bfloat16)], axis=1)
    high = jnp.concatenate([block[:, half:] for block in blocks] + [counts.astype(jnp.bfloat16)], axis=1)
    first = place_ref[0] == 0
    send_ref[:rows, :] = images_ref[...]
    send_ref[rows:, :] = jnp.where(first, high, low)
    keep_ref[...] = jnp.where(first, low, high)


def norm_kernel(images_ref, keep_ref, came_ref, gain_ref, bias_ref, out_ref):
    gain, bias = gain_ref[...].reshape(1, -1), bias_ref[...].reshape(1, -1)
    rows = images_ref.shape[0]
    for index, source in enumerate((images_ref, came_ref)):
        for start in range(0, rows, CHUNK):
            values = source[start : start + CHUNK, :].astype(jnp.float32)
            centre = values - jnp.mean(values, axis=-1, keepdims=True)
            spread = jnp.mean(centre * centre, axis=-1, keepdims=True)
            normed = centre * lax.rsqrt(spread + EPSILON) * gain + bias
            out_ref[index, start : start + CHUNK, :] = normed.astype(jnp.bfloat16)
    out_ref[0, rows:, :] = keep_ref[...]
    out_ref[1, rows:, :] = came_ref[rows:, :]


def across(left, right):
    return lax.dot_general(left, right, (((1,), (1,)), ((), ())), preferred_element_type=jnp.float32)


def along(left, right):
    return lax.dot_general(left, right, (((0,), (0,)), ((), ())), preferred_element_type=jnp.float32)


def plain(left, right):
    return jnp.dot(left, right, preferred_element_type=jnp.float32)


def one_hot(chosen):
    return jnp.where(chosen, 1.0, 0.0).astype(jnp.bfloat16)


def iota(shape, axis):
    return lax.broadcasted_iota(jnp.int32, shape, axis)


def column_order(piece, quarter):
    row, out = iota((4 * LANES, 6 * LANES), 0), iota((4 * LANES, 6 * LANES), 1)
    kind = (out >= 2 * LANES).astype(jnp.int32) + (out >= 4 * LANES).astype(jnp.int32)
    lane = out - 2 * LANES * kind
    block = sum((lane >= piece * n).astype(jnp.int32) for n in (1, 2, 3))
    source = LANES * block + piece * kind + lane - piece * block
    return one_hot((row == source) & (lane < quarter))


def main_kernel(
    slots, latent_count, ring, sharers,
    index_ref, near_ref, far_ref, whole_ref, query_ref,
    lat_ref, lat_c_ref, packed_ref,
    weight_ref, grad_ref, total_ref, tail_ref,
):
    width_in = near_ref.shape[2]
    rows = near_ref.shape[1] - latent_count
    capacity = rows // slots
    quarter = lat_ref.shape[2]
    head_size = quarter // HEADS
    scale = 1.0 / math.sqrt(head_size)
    for block in range(4):
        halves = [whole_ref[4 * half + block].astype(jnp.float32) for half in range(2)]
        stacked = jnp.stack(halves, axis=1).reshape(width_in, LANES)
        weight_ref[:, LANES * block : LANES * (block + 1)] = stacked.astype(jnp.bfloat16)
    order = column_order(quarter // 4, quarter)
    first_head = iota((1, quarter), 1) < head_size
    nothing = jnp.zeros((), jnp.bfloat16)

    def head_of(array, head):
        return jnp.where(first_head, array, nothing) if head == 0 else jnp.where(first_head, nothing, array)

    def both_heads(array):
        return jnp.concatenate([head_of(array, 0), head_of(array, 1)], axis=0)

    width = query_ref.shape[1]
    pick = one_hot(
        (iota((width, 2 * LANES), 0) == quarter * index_ref[0] + iota((width, 2 * LANES), 1))
        & (iota((width, 2 * LANES), 1) < quarter)
    )
    query = both_heads(plain(query_ref[...], pick).astype(jnp.bfloat16)[:, :quarter])
    grad_ref[...] = jnp.zeros_like(grad_ref)
    image_of = [
        sum((iota(shape, axis) >= capacity * n).astype(jnp.int32) for n in range(1, slots))
        for shape, axis in (((rows, 1), 0), ((1, rows), 1))
    ]
    place = [
        (iota(shape, axis) - capacity * image).astype(jnp.float32)
        for (shape, axis), image in zip((((rows, 1), 0), ((1, rows), 1)), image_of)
    ]
    members = [ref.at[n] for ref in (near_ref, far_ref) for n in range(ref.shape[0])]
    first_pair = index_ref[0] % 2 == 0
    outs = [ref.at[n] for ref in (lat_ref, lat_c_ref) for n in range(ref.shape[0])]
    apart = slots, capacity, HEADS * latent_count

    def limits(block):
        sizes = members[block][rows : rows + 16, 2 * quarter * slots :].astype(jnp.float32)
        size = [sizes[n : n + 1, 0:1] for n in range(slots)]
        live = []
        for image, position in zip(image_of, place):
            limit = size[slots - 1] + jnp.zeros_like(position)
            for n in reversed(range(slots - 1)):
                limit = jnp.where(image == n, size[n], limit)
            live.append(position < limit)
        return jnp.where(live[0], image_of[0], -1), jnp.where(live[1], image_of[1], -2)

    def attention(scores, allowed):
        scores = jnp.where(allowed, scores * scale, MASKED)
        highest = jnp.max(scores, axis=-1, keepdims=True)
        raised = jnp.where(allowed, jnp.exp(scores - highest), 0.0)
        total = jnp.maximum(jnp.sum(raised, axis=-1, keepdims=True), 1.0)
        return (raised * (1.0 / total)).astype(jnp.bfloat16)

    def over_patches(scores, labels):
        inside = (labels[0] >= 0).reshape(slots, capacity, 1)
        masked = jnp.where(inside, scores.reshape(apart) * scale, MASKED)
        raised = jnp.where(inside, jnp.exp(masked - jnp.max(masked, axis=1, keepdims=True)), 0.0)
        return raised * (1.0 / jnp.maximum(jnp.sum(raised, axis=1, keepdims=True), 1.0))

    def normed(block):
        return members[block][:rows, :]

    def cotangent_of(block, n):
        ride = members[block][rows:, 2 * quarter * n : 2 * quarter * (n + 1)]
        return both_heads(jnp.where(first_pair, ride[:, :quarter], ride[:, quarter:]))

    def span(n):
        return slice(latent_count * n, latent_count * (n + 1))

    for first in range(0, len(members), WAVE):
        blocks = range(first, min(first + WAVE, len(members)))
        labels = [limits(b) for b in blocks]
        projected = [plain(normed(b), weight_ref[...]).astype(jnp.bfloat16) for b in blocks]
        parts = [plain(p, order).astype(jnp.bfloat16) for p in projected]
        parts = [[p[:, 2 * LANES * n : 2 * LANES * n + quarter] for n in range(3)] for p in parts]
        scores = [[across(head_of(q, h), k) for h in range(HEADS)] for q, k, _ in parts]
        weights = [[attention(s, m[0] == m[1]) for s in both] for both, m in zip(scores, labels)]
        mixed = [
            sum(plain(w[h], head_of(v, h)) for h in range(HEADS)).astype(jnp.bfloat16)
            for w, (_, _, v) in zip(weights, parts)
        ]
        shares = [over_patches(across(m, query), l) for m, l in zip(mixed, labels)]
        low = [s.astype(jnp.bfloat16) for s in shares]
        split = [m.reshape(slots, capacity, quarter) for m in mixed]
        cotangent = [[cotangent_of(b, n) for n in range(slots)] for b in blocks]
        share_grads = [
            jnp.stack([across(s[n], g[n]) for n in range(slots)]) for s, g in zip(split, cotangent)
        ]
        for b, l, s in zip(blocks, low, split):
            for n in range(slots):
                latents = along(l[n], s[n])
                outs[b][span(n), :] = jnp.where(first_head, latents[:latent_count], latents[latent_count:])
        score_grads = [
            s * (g - jnp.sum(s * g, axis=1, keepdims=True)) * scale for s, g in zip(shares, share_grads)
        ]
        score_grads = [g.reshape(rows, HEADS * latent_count) for g in score_grads]
        high = [g.astype(jnp.bfloat16) for g in score_grads]
        rest = [(g - h.astype(jnp.float32)).astype(jnp.bfloat16) for g, h in zip(score_grads, high)]
        from_values = [
            jnp.concatenate([plain(l[n], g[n]) for n in range(slots)], axis=0) for l, g in zip(low, cotangent)
        ]
        mixed_grad = [
            (v + (plain(h, query) + plain(r, query))).astype(jnp.bfloat16)
            for v, h, r in zip(from_values, high, rest)
        ]
        for b, w, g in zip(blocks, weights, mixed_grad):
            value_grad = sum(along(w[h], head_of(g, h)) for h in range(HEADS))
            grad_ref[rows * b : rows * (b + 1), :quarter] = value_grad.astype(jnp.bfloat16)
    total = sum(
        along(grad_ref[rows * b : rows * (b + 1), :], normed(b)) for b in range(len(members))
    )
    total_ref[...] = total[:LANES].T
    tail_ref[...] = total[LANES:].T
    depth = width_in // ring
    part = depth // sharers
    per_tile = LANES // (quarter - LANES)
    for sharer in range(sharers):
        rest = []
        for row in range(part):
            picked = pl.ds(sharer * part + row, ring, stride=depth)
            packed_ref[sharer, :, LANES * row : LANES * (row + 1)] = total_ref[picked, :].astype(jnp.bfloat16)
            tail = tail_ref[picked, :]
            shift = (row % per_tile) * (quarter - LANES)
            if shift == 0:
                rest.append(tail)
            else:
                rest[-1] = rest[-1] + pltpu.roll(tail, shift, 1)
        for n, tile in enumerate(rest):
            lanes = slice(LANES * (part + n), LANES * (part + n + 1))
            packed_ref[sharer, :, lanes] = tile.astype(jnp.bfloat16)


def order_kernel(index_ref, own_ref, x_ref, out_ref, parts_ref):
    quarter = own_ref.shape[2]
    parts_ref[:2] = own_ref[...]
    parts_ref[2:] = x_ref[...]
    for pair in range(4):
        out_ref[:, quarter * pair : quarter * (pair + 1)] = parts_ref[pair ^ index_ref[0]]


def call(kernel, outs, scratch, flops, *operands, limit=24):
    memory = pl.BlockSpec(memory_space=pltpu.VMEM)
    scalars = pl.BlockSpec(memory_space=pltpu.SMEM)
    size = sum(math.prod(a.shape) * a.dtype.itemsize for a in (*operands, *outs))
    return pl.pallas_call(
        kernel,
        out_shape=outs,
        in_specs=[scalars if a.dtype == jnp.int32 else memory for a in operands],
        out_specs=[memory] * len(outs),
        scratch_shapes=scratch,
        compiler_params=pltpu.CompilerParams(vmem_limit_bytes=limit * MIB),
        cost_estimate=pl.CostEstimate(flops=flops, bytes_accessed=size, transcendentals=0),
    )(*operands)


def pack(place, counts, images, grads):
    below = grads.shape[0] // counts.shape[0]
    send = jax.ShapeDtypeStruct((images.shape[0] + below, images.shape[1]), jnp.bfloat16)
    keep = jax.ShapeDtypeStruct((below, images.shape[1]), jnp.bfloat16)
    return call(pack_kernel, [send, keep], [], images.size, place, counts, images, grads, limit=56)


def layer_norm(images, keep, came, gain, bias):
    out = jax.ShapeDtypeStruct((2,) + came.shape, jnp.bfloat16)
    return call(norm_kernel, [out], [], 40 * images.size, images, keep, came, gain, bias)[0]


def attend(index, near, far, whole, query, slots, latent_count, ring):
    width_in = near.shape[2]
    rows = near.shape[1] - latent_count
    quarter = query.shape[1] // 4
    sharers = whole.shape[0]
    part = width_in // ring // sharers
    packed = LANES * (part + -(-part * (quarter - LANES) // LANES))
    latents = jax.ShapeDtypeStruct((2, slots * latent_count, quarter), jnp.float32)
    return call(
        functools.partial(main_kernel, slots, latent_count, ring, sharers),
        [latents, latents, jax.ShapeDtypeStruct((sharers, ring, packed), jnp.bfloat16)],
        [
            pltpu.VMEM((width_in, 4 * LANES), jnp.bfloat16),
            pltpu.VMEM((4 * rows, 2 * LANES), jnp.bfloat16),
            pltpu.VMEM((width_in, LANES), jnp.float32),
            pltpu.VMEM((width_in, LANES), jnp.float32),
        ],
        2 * 4 * rows * width_in * 5 * quarter,
        index, near, far, whole, query,
    )


def copies(piece, count):
    return jnp.broadcast_to(piece[None], (count,) + piece.shape)


def exchange(array, axes):
    return lax.all_to_all(array, axes, 0, 0, tiled=True)


def unpack(packed, part, quarter):
    lead = packed.shape[:-1]
    head = packed[..., : LANES * part].reshape(lead + (part, LANES))
    rest = packed[..., LANES * part : LANES * part + part * (quarter - LANES)]
    return jnp.concatenate([head, rest.reshape(lead + (part, quarter - LANES))], axis=-1)


def on_device(patches, counts, norm_gain, norm_bias, input_weight, latent_query, cotangent):
    slots, capacity, width_in = patches.shape[2:]
    latent_count, width = cotangent.shape[3:]
    depth = input_weight.shape[0]
    ring = lax.axis_size("z")
    sharers = lax.axis_size(PLANE)
    xp, xi, y, c = (lax.axis_index(a) for a in DP)
    pair = 2 * xi + c
    quarter = width // 4

    images = patches.reshape(slots * capacity, width_in)
    grads = cotangent.reshape(slots * latent_count, width)
    send, keep = pack(xi.astype(jnp.int32).reshape(1), counts.reshape(slots), images, grads)
    came = lax.ppermute(send, "xi", SWAP)

    piece = quarter // 4
    rows = lax.dynamic_slice_in_dim(input_weight, xp * (depth // 2), depth // 2, 0)
    target = jnp.arange(LANES, dtype=jnp.int32)
    source = width * (target // piece) + quarter * pair + piece * y + target % piece
    source = jnp.where(target < 3 * piece, source, -1)
    pick = (jnp.arange(3 * width, dtype=jnp.int32)[:, None] == source[None, :]).astype(jnp.bfloat16)
    own = jnp.dot(rows, pick, preferred_element_type=jnp.float32).astype(jnp.bfloat16)
    gathered = exchange(copies(own, ring), "z")

    normed = layer_norm(images, keep, came, norm_gain, norm_bias)
    normed_c = lax.ppermute(normed, "c", SWAP)
    gathered, _ = lax.optimization_barrier((gathered, normed))

    whole = exchange(copies(gathered, sharers), PLANE)
    index = pair.astype(jnp.int32).reshape(1)
    latents, latents_c, packed = attend(
        index, normed, normed_c, whole, latent_query, slots, latent_count, ring
    )

    part = depth // sharers
    came = exchange(packed, PLANE).astype(jnp.float32)
    summed = jnp.sum(came.reshape(sharers, ring, 1, -1), axis=0)
    both = jnp.stack([latents, lax.ppermute(latents_c, "c", SWAP)], axis=1)
    summed = jnp.sum(exchange(summed, "z"), axis=0)
    latents_x = lax.ppermute(both[1], "xi", SWAP)
    done = unpack(exchange(copies(summed, 4 * sharers), DP)[:, 0], part, quarter)
    grad_value = (
        done.reshape(2, 2, 4, 2, part, quarter).transpose(0, 2, 4, 1, 3, 5).reshape(depth, width)
    )

    shape = jax.ShapeDtypeStruct((slots * latent_count, width), jnp.float32)
    parts = pltpu.VMEM((4,) + latents.shape[1:], jnp.float32)
    latents = call(order_kernel, [shape], [parts], both.size, index, both[0], latents_x)[0]
    return latents.reshape(cotangent.shape), grad_value


def solution(mesh):
    fine = Mesh(mesh.devices.reshape(2, 2, 4, 2, 16), DP + ("z",))
    placed = (
        P(DP, "z", None, None, None),
        P(DP, "z", None),
        P(),
        P(),
        P("z", None),
        P(),
        P(DP, "z", None, None, None),
    )
    return jax.shard_map(
        on_device,
        mesh=fine,
        in_specs=placed,
        out_specs=(P(DP, "z", None, None, None), P("z", None)),
        check_vma=False,
    )
```

```python
import functools
import math

import jax
import jax.numpy as jnp
from jax import lax
from jax.experimental import pallas as pl
from jax.experimental.pallas import tpu as pltpu
from jax.sharding import Mesh
from jax.sharding import PartitionSpec as P

HEADS = 2
EPSILON = 1e-06
MASKED = -1e30
DP = ("x", "y", "c")
PLANE = ("x", "y")
RING = ("zh", "zl")
SWAP = [(0, 1), (1, 0)]
LANES = 128
CHUNK = 16
WAVE = 4
MIB = 1024 * 1024


def pack_kernel(place_ref, counts_ref, images_ref, grads_ref, send_ref, keep_ref):
    rows, half = images_ref.shape[0], grads_ref.shape[1] // 2
    slots = counts_ref.shape[0]
    latent_count = grads_ref.shape[0] // slots
    row = iota((latent_count, half), 0)
    counts = jnp.zeros((latent_count, half), jnp.float32)
    for n in range(slots):
        counts = jnp.where(row == n, counts_ref[n].astype(jnp.float32), counts)
    blocks = [grads_ref[latent_count * n : latent_count * (n + 1), :] for n in range(slots)]
    low = jnp.concatenate([block[:, :half] for block in blocks] + [counts.astype(jnp.bfloat16)], axis=1)
    high = jnp.concatenate([block[:, half:] for block in blocks] + [counts.astype(jnp.bfloat16)], axis=1)
    first = place_ref[0] == 0
    send_ref[:rows, :] = images_ref[...]
    send_ref[rows:, :] = jnp.where(first, high, low)
    keep_ref[...] = jnp.where(first, low, high)


def norm_kernel(rows_ref, below_ref, gain_ref, bias_ref, out_ref):
    gain, bias = gain_ref[...].reshape(1, -1), bias_ref[...].reshape(1, -1)
    rows = out_ref.shape[0] - below_ref.shape[0]
    for start in range(0, rows, CHUNK):
        values = rows_ref[start : start + CHUNK, :].astype(jnp.float32)
        centre = values - jnp.mean(values, axis=-1, keepdims=True)
        spread = jnp.mean(centre * centre, axis=-1, keepdims=True)
        normed = centre * lax.rsqrt(spread + EPSILON) * gain + bias
        out_ref[start : start + CHUNK, :] = normed.astype(jnp.bfloat16)
    out_ref[rows:, :] = below_ref[...]


def norm_came_kernel(came_ref, gain_ref, bias_ref, out_ref, *, below):
    rows = out_ref.shape[0] - below
    norm_kernel(came_ref.at[:rows], came_ref.at[rows:], gain_ref, bias_ref, out_ref)


def across(left, right):
    return lax.dot_general(left, right, (((1,), (1,)), ((), ())), preferred_element_type=jnp.float32)


def along(left, right):
    return lax.dot_general(left, right, (((0,), (0,)), ((), ())), preferred_element_type=jnp.float32)


def plain(left, right):
    return jnp.dot(left, right, preferred_element_type=jnp.float32)


def one_hot(chosen):
    return jnp.where(chosen, 1.0, 0.0).astype(jnp.bfloat16)


def iota(shape, axis):
    return lax.broadcasted_iota(jnp.int32, shape, axis)


def columns(projected, piece, start, stop):
    span = 3 * piece
    parts = []
    for tile in range(start // span, (stop - 1) // span + 1):
        low, high = max(start - span * tile, 0), min(stop - span * tile, span)
        parts.append(projected[:, LANES * tile + low : LANES * tile + high])
    return jnp.concatenate(parts, axis=1)


def main_kernel(
    slots, latent_count, ring, sharers,
    indepartner_ref, own_ref, partner_ref, own_c_ref, partner_c_ref, whole_ref, query_ref,
    lat_ref, lat_c_ref, packed_ref,
    held_ref, arrived, weight_ref, grad_ref, total_ref, tail_ref,
):
    width_in = own_ref.shape[1]
    rows = own_ref.shape[0] - latent_count
    fetched = [
        pltpu.make_async_copy(ref, held_ref.at[n], arrived.at[n])
        for n, ref in enumerate((own_ref, partner_ref, own_c_ref, partner_c_ref))
    ]
    for copy in fetched:
        copy.start()
    capacity = rows // slots
    quarter = lat_ref.shape[2]
    head_size = quarter // HEADS
    scale = 1.0 / math.sqrt(head_size)
    strip = width_in // ring // 4
    for block in range(4):
        for part in range(4):
            strips = whole_ref[4 * part + block].astype(jnp.float32)
            for step in range(ring):
                start = strip * (4 * step + part)
                total_ref[start : start + strip, :] = strips[step, :strip]
        weight_ref[:, LANES * block : LANES * (block + 1)] = total_ref[...].astype(jnp.bfloat16)
    first_head = iota((1, quarter), 1) < head_size
    nothing = jnp.zeros((), jnp.bfloat16)

    def head_of(array, head):
        return jnp.where(first_head, array, nothing) if head == 0 else jnp.where(first_head, nothing, array)

    def both_heads(array):
        return jnp.concatenate([head_of(array, 0), head_of(array, 1)], axis=0)

    width = query_ref.shape[1]
    pick = one_hot(
        (iota((width, 2 * LANES), 0) == quarter * indepartner_ref[0] + iota((width, 2 * LANES), 1))
        & (iota((width, 2 * LANES), 1) < quarter)
    )
    query = both_heads(plain(query_ref[...], pick).astype(jnp.bfloat16)[:, :quarter])
    tail_ref[...] = jnp.zeros_like(tail_ref)
    image_of = [
        sum((iota(shape, axis) >= capacity * n).astype(jnp.int32) for n in range(1, slots))
        for shape, axis in (((rows, 1), 0), ((1, rows), 1))
    ]
    place = [
        (iota(shape, axis) - capacity * image).astype(jnp.float32)
        for (shape, axis), image in zip((((rows, 1), 0), ((1, rows), 1)), image_of)
    ]
    members = [held_ref.at[n] for n in range(4)]
    first_pair = indepartner_ref[0] % 2 == 0
    outs = [ref.at[n] for ref in (lat_ref, lat_c_ref) for n in range(ref.shape[0])]
    apart = slots, capacity, HEADS * latent_count

    def limits(block):
        sizes = members[block][rows : rows + 16, 2 * quarter * slots :].astype(jnp.float32)
        size = [sizes[n : n + 1, 0:1] for n in range(slots)]
        live = []
        for image, position in zip(image_of, place):
            limit = size[slots - 1] + jnp.zeros_like(position)
            for n in reversed(range(slots - 1)):
                limit = jnp.where(image == n, size[n], limit)
            live.append(position < limit)
        return jnp.where(live[0], image_of[0], -1), jnp.where(live[1], image_of[1], -2)

    def attention(scores, allowed):
        scores = jnp.where(allowed, scores * scale, MASKED)
        highest = jnp.max(scores, axis=-1, keepdims=True)
        raised = jnp.exp(scores - highest)
        total = jnp.maximum(jnp.sum(raised, axis=-1, keepdims=True), 1.0)
        return (raised * (1.0 / total)).astype(jnp.bfloat16)

    def over_patches(scores, labels):
        inside = (labels[0] >= 0).reshape(slots, capacity, 1)
        masked = jnp.where(inside, scores.reshape(apart) * scale, MASKED)
        raised = jnp.where(inside, jnp.exp(masked - jnp.max(masked, axis=1, keepdims=True)), 0.0)
        return raised * (1.0 / jnp.maximum(jnp.sum(raised, axis=1, keepdims=True), 1.0))

    def normed(block):
        return members[block][:rows, :]

    def cotangent_of(block, n):
        ride = members[block][rows:, 2 * quarter * n : 2 * quarter * (n + 1)]
        return both_heads(jnp.where(first_pair, ride[:, :quarter], ride[:, quarter:]))

    def span(n):
        return slice(latent_count * n, latent_count * (n + 1))

    for copy in fetched:
        copy.wait()
    for first in range(0, len(members), WAVE):
        blocks = range(first, min(first + WAVE, len(members)))
        labels = [limits(b) for b in blocks]
        projected = [plain(normed(b), weight_ref[...]).astype(jnp.bfloat16) for b in blocks]
        parts = [
            [columns(p, quarter // 4, quarter * n, quarter * (n + 1)) for n in range(3)] for p in projected
        ]
        scores = [[across(head_of(q, h), k) for h in range(HEADS)] for q, k, _ in parts]
        weights = [[attention(s, m[0] == m[1]) for s in both] for both, m in zip(scores, labels)]
        mixed = [
            sum(plain(w[h], head_of(v, h)) for h in range(HEADS)).astype(jnp.bfloat16)
            for w, (_, _, v) in zip(weights, parts)
        ]
        shares = [over_patches(across(m, query), l) for m, l in zip(mixed, labels)]
        low = [s.astype(jnp.bfloat16) for s in shares]
        split = [m.reshape(slots, capacity, quarter) for m in mixed]
        cotangent = [[cotangent_of(b, n) for n in range(slots)] for b in blocks]
        share_grads = [
            jnp.stack([across(s[n], g[n]) for n in range(slots)]) for s, g in zip(split, cotangent)
        ]
        for b, l, s in zip(blocks, low, split):
            for n in range(slots):
                latents = along(l[n], s[n])
                outs[b][span(n), :] = jnp.where(first_head, latents[:latent_count], latents[latent_count:])
        score_grads = [
            s * (g - jnp.sum(s * g, axis=1, keepdims=True)) * scale for s, g in zip(shares, share_grads)
        ]
        score_grads = [g.reshape(rows, HEADS * latent_count) for g in score_grads]
        high = [g.astype(jnp.bfloat16) for g in score_grads]
        rest = [(g - h.astype(jnp.float32)).astype(jnp.bfloat16) for g, h in zip(score_grads, high)]
        from_values = [
            jnp.concatenate([plain(l[n], g[n]) for n in range(slots)], axis=0) for l, g in zip(low, cotangent)
        ]
        mixed_grad = [
            (v + (plain(h, query) + plain(r, query))).astype(jnp.bfloat16)
            for v, h, r in zip(from_values, high, rest)
        ]
        for b, w, g in zip(blocks, weights, mixed_grad):
            value_grad = sum(along(w[h], head_of(g, h)) for h in range(HEADS))
            grad_ref[rows * b : rows * (b + 1), :] = value_grad.astype(jnp.bfloat16)
    total = sum(
        along(grad_ref[rows * b : rows * (b + 1), :], normed(b)) for b in range(len(members))
    )
    total_ref[...] = total[:LANES].T
    tail_ref[:, : quarter - LANES] = total[LANES:].T
    depth = width_in // ring
    part = depth // sharers
    per_tile = LANES // (quarter - LANES)
    for sharer in range(sharers):
        rest = []
        for row in range(part):
            picked = pl.ds(sharer * part + row, ring, stride=depth)
            packed_ref[sharer, :, LANES * row : LANES * (row + 1)] = total_ref[picked, :].astype(jnp.bfloat16)
            tail = tail_ref[picked, :]
            shift = (row % per_tile) * (quarter - LANES)
            if shift == 0:
                rest.append(tail)
            else:
                rest[-1] = rest[-1] + pltpu.roll(tail, shift, 1)
        for n, tile in enumerate(rest):
            lanes = slice(LANES * (part + n), LANES * (part + n + 1))
            packed_ref[sharer, :, lanes] = tile.astype(jnp.bfloat16)


def order_kernel(indepartner_ref, own_ref, partner_ref, out_ref, parts_ref):
    quarter = own_ref.shape[2]
    parts_ref[:2] = own_ref[...]
    parts_ref[2:] = partner_ref[...]
    for pair in range(4):
        out_ref[:, quarter * pair : quarter * (pair + 1)] = parts_ref[pair ^ indepartner_ref[0]]


def call(kernel, outs, scratch, flops, *operands, limit=24, unplaced=()):
    memory = pl.BlockSpec(memory_space=pltpu.VMEM)
    scalars = pl.BlockSpec(memory_space=pltpu.SMEM)
    size = sum(math.prod(a.shape) * a.dtype.itemsize for a in (*operands, *outs))
    return pl.pallas_call(
        kernel,
        out_shape=outs,
        in_specs=[
            pl.BlockSpec(memory_space=pl.ANY) if n in unplaced else scalars if a.dtype == jnp.int32 else memory
            for n, a in enumerate(operands)
        ],
        out_specs=[memory] * len(outs),
        scratch_shapes=scratch,
        compiler_params=pltpu.CompilerParams(vmem_limit_bytes=limit * MIB),
        cost_estimate=pl.CostEstimate(flops=flops, bytes_accessed=size, transcendentals=0),
    )(*operands)


def pack(place, counts, images, grads):
    below = grads.shape[0] // counts.shape[0]
    send = jax.ShapeDtypeStruct((images.shape[0] + below, images.shape[1]), jnp.bfloat16)
    keep = jax.ShapeDtypeStruct((below, images.shape[1]), jnp.bfloat16)
    return call(pack_kernel, [send, keep], [], images.size, place, counts, images, grads, limit=56)


def layer_norm(rows, below, gain, bias):
    out = jax.ShapeDtypeStruct((rows.shape[0] + below.shape[0], rows.shape[1]), jnp.bfloat16)
    return call(norm_kernel, [out], [], 20 * rows.size, rows, below, gain, bias)[0]


def layer_norm_came(came, below, gain, bias):
    out = jax.ShapeDtypeStruct(came.shape, jnp.bfloat16)
    kernel = functools.partial(norm_came_kernel, below=below)
    return call(kernel, [out], [], 20 * came.size, came, gain, bias)[0]


def attend(index, members, whole, query, slots, latent_count, ring):
    width_in = members[0].shape[1]
    rows = members[0].shape[0] - latent_count
    quarter = query.shape[1] // 4
    sharers = whole.shape[0]
    part = width_in // ring // sharers
    packed = LANES * (part + -(-part * (quarter - LANES) // LANES))
    latents = jax.ShapeDtypeStruct((2, slots * latent_count, quarter), jnp.float32)
    return call(
        functools.partial(main_kernel, slots, latent_count, ring, sharers),
        [latents, latents, jax.ShapeDtypeStruct((sharers, ring, packed), jnp.bfloat16)],
        [
            pltpu.VMEM((4,) + members[0].shape, jnp.bfloat16),
            pltpu.SemaphoreType.DMA((4,)),
            pltpu.VMEM((width_in, 4 * LANES), jnp.bfloat16),
            pltpu.VMEM((4 * rows, quarter), jnp.bfloat16),
            pltpu.VMEM((width_in, LANES), jnp.float32),
            pltpu.VMEM((width_in, LANES), jnp.float32),
        ],
        2 * 4 * rows * width_in * 5 * quarter,
        index, *members, whole, query, unplaced=(1, 2, 3, 4), limit=56,
    )


def copies(piece, count):
    return jnp.broadcast_to(piece[None], (count,) + piece.shape)


def exchange(array, axes):
    return lax.all_to_all(array, axes, 0, 0, tiled=True)


def unpack(packed, part, quarter):
    lead = packed.shape[:-1]
    head = packed[..., : LANES * part].reshape(lead + (part, LANES))
    rest = packed[..., LANES * part : LANES * part + part * (quarter - LANES)]
    return jnp.concatenate([head, rest.reshape(lead + (part, quarter - LANES))], axis=-1)


def on_device(patches, counts, norm_gain, norm_bias, input_weight, latent_query, cotangent):
    slots, capacity, width_in = patches.shape[2:]
    latent_count, width = cotangent.shape[3:]
    depth = input_weight.shape[0]
    ring = lax.axis_size(RING)
    sharers = lax.axis_size(PLANE)
    x, y, c = (lax.axis_index(a) for a in DP)
    near_z = lax.axis_index("zl")
    pair = 2 * near_z + c
    quarter = width // 4

    images = patches.reshape(slots * capacity, width_in)
    grads = cotangent.reshape(slots * latent_count, width)
    send, keep = pack(near_z.astype(jnp.int32).reshape(1), counts.reshape(slots), images, grads)
    came = lax.ppermute(send, "zl", SWAP)

    piece = quarter // 4
    strip = depth // 4
    rows = lax.dynamic_slice_in_dim(input_weight, x * strip, strip, 0)
    target = jnp.arange(2 * LANES, dtype=jnp.int32)
    column = 3 * piece * y + target % LANES
    source = width * (column // quarter) + quarter * (2 * (target // LANES) + c) + column % quarter
    source = jnp.where(target % LANES < 3 * piece, source, -1)
    pick = (jnp.arange(3 * width, dtype=jnp.int32)[:, None] == source[None, :]).astype(jnp.bfloat16)
    own = jnp.dot(rows, pick, preferred_element_type=jnp.float32).astype(jnp.bfloat16)
    own = jnp.pad(jnp.stack([own[:, :LANES], own[:, LANES:]]), ((0, 0), (0, 4), (0, 0)))
    pieces = copies(own, ring // 2).reshape(ring, strip + 4, LANES)
    gathered = exchange(pieces, RING)

    own_rows = layer_norm(images, keep, norm_gain, norm_bias)
    own_c = lax.ppermute(own_rows, "c", SWAP)
    came_rows = layer_norm_came(came, keep.shape[0], norm_gain, norm_bias)
    came_c = lax.ppermute(came_rows, "c", SWAP)

    whole = exchange(copies(gathered, sharers), PLANE)
    index = pair.astype(jnp.int32).reshape(1)
    latents, latents_c, packed = attend(
        index, (own_rows, came_rows, own_c, came_c), whole, latent_query, slots, latent_count, ring
    )

    part = depth // sharers
    came = exchange(packed, PLANE).astype(jnp.float32)
    summed = jnp.sum(came.reshape(sharers, ring, 1, -1), axis=0)
    both = jnp.stack([latents, lax.ppermute(latents_c, "c", SWAP)], axis=1)
    summed = exchange(summed, RING)
    summed = jnp.sum(summed.reshape(ring // 2, 2, -1), axis=0)
    latents_z = lax.ppermute(both[1], "zl", SWAP)
    done = unpack(exchange(copies(summed, 2 * sharers), DP), part, quarter)
    done = done.reshape(4, 4, 2, 2, part, quarter).transpose(0, 1, 4, 3, 2, 5)
    grad_value = done.reshape(depth, width)

    shape = jax.ShapeDtypeStruct((slots * latent_count, width), jnp.float32)
    parts = pltpu.VMEM((4,) + latents.shape[1:], jnp.float32)
    latents = call(order_kernel, [shape], [parts], both.size, index, both[0], latents_z)[0]
    return latents.reshape(cotangent.shape), grad_value


def solution(mesh):
    fine = Mesh(mesh.devices.reshape(4, 4, 2, 8, 2), DP + RING)
    placed = (
        P(DP, RING, None, None, None),
        P(DP, RING, None),
        P(),
        P(),
        P(RING, None),
        P(),
        P(DP, RING, None, None, None),
    )
    return jax.shard_map(
        on_device,
        mesh=fine,
        in_specs=placed,
        out_specs=(P(DP, RING, None, None, None), P(RING, None)),
        check_vma=False,
    )
```

```python
import functools
import math

import jax
import jax.numpy as jnp
from jax import lax
from jax.experimental import pallas as pl
from jax.experimental.pallas import tpu as pltpu
from jax.sharding import Mesh
from jax.sharding import PartitionSpec as P

HEADS = 2
EPSILON = 1e-06
MASKED = -1e30
DP = ("x", "y", "c")
PLANE = ("x", "y")
RING = ("zh", "zl")
SWAP = [(0, 1), (1, 0)]
LANES = 128
CHUNK = 16
WAVE = 4
MIB = 1024 * 1024


def pack_kernel(place_ref, counts_ref, images_ref, grads_ref, send_ref, keep_ref):
    rows, half = images_ref.shape[0], grads_ref.shape[1] // 2
    slots = counts_ref.shape[0]
    latent_count = grads_ref.shape[0] // slots
    row = iota((latent_count, half), 0)
    counts = jnp.zeros((latent_count, half), jnp.float32)
    for n in range(slots):
        counts = jnp.where(row == n, counts_ref[n].astype(jnp.float32), counts)
    blocks = [grads_ref[latent_count * n : latent_count * (n + 1), :] for n in range(slots)]
    low = jnp.concatenate([block[:, :half] for block in blocks] + [counts.astype(jnp.bfloat16)], axis=1)
    high = jnp.concatenate([block[:, half:] for block in blocks] + [counts.astype(jnp.bfloat16)], axis=1)
    first = place_ref[0] == 0
    send_ref[:rows, :] = images_ref[...]
    send_ref[rows:, :] = jnp.where(first, high, low)
    keep_ref[...] = jnp.where(first, low, high)


def norm_kernel(rows_ref, below_ref, gain_ref, bias_ref, out_ref):
    gain, bias = gain_ref[...].reshape(1, -1), bias_ref[...].reshape(1, -1)
    rows = out_ref.shape[0] - below_ref.shape[0]
    for start in range(0, rows, CHUNK):
        values = rows_ref[start : start + CHUNK, :].astype(jnp.float32)
        centre = values - jnp.mean(values, axis=-1, keepdims=True)
        spread = jnp.mean(centre * centre, axis=-1, keepdims=True)
        normed = centre * lax.rsqrt(spread + EPSILON) * gain + bias
        out_ref[start : start + CHUNK, :] = normed.astype(jnp.bfloat16)
    out_ref[rows:, :] = below_ref[...]


def norm_came_kernel(came_ref, gain_ref, bias_ref, out_ref, *, below):
    rows = out_ref.shape[0] - below
    norm_kernel(came_ref.at[:rows], came_ref.at[rows:], gain_ref, bias_ref, out_ref)


def spread_kernel(in_ref, out_ref, flat_ref):
    ring = in_ref.shape[0]
    strip = flat_ref.shape[0] // ring
    for step in range(ring):
        flat_ref[strip * step : strip * (step + 1), :] = in_ref[step].astype(jnp.float32)[:strip]
    flat = flat_ref[...].astype(jnp.bfloat16)
    for receiver in range(out_ref.shape[0]):
        out_ref[receiver] = flat


def plane_sum_kernel(in_ref, out_ref):
    total = sum(in_ref[n].astype(jnp.float32) for n in range(in_ref.shape[0]))
    for step in range(out_ref.shape[0]):
        out_ref[step] = total[step : step + 1, :]


def ring_sum_kernel(in_ref, out_ref):
    kinds = [sum(in_ref[n] for n in range(kind, in_ref.shape[0], 2)) for kind in range(2)]
    pair = jnp.concatenate(kinds, axis=0)
    for receiver in range(out_ref.shape[0]):
        out_ref[receiver] = pair


def across(left, right):
    return lax.dot_general(left, right, (((1,), (1,)), ((), ())), preferred_element_type=jnp.float32)


def along(left, right):
    return lax.dot_general(left, right, (((0,), (0,)), ((), ())), preferred_element_type=jnp.float32)


def plain(left, right):
    return jnp.dot(left, right, preferred_element_type=jnp.float32)


def one_hot(chosen):
    return jnp.where(chosen, 1.0, 0.0).astype(jnp.bfloat16)


def iota(shape, axis):
    return lax.broadcasted_iota(jnp.int32, shape, axis)


def columns(projected, piece, start, stop):
    span = 3 * piece
    parts = []
    for tile in range(start // span, (stop - 1) // span + 1):
        low, high = max(start - span * tile, 0), min(stop - span * tile, span)
        parts.append(projected[:, LANES * tile + low : LANES * tile + high])
    return jnp.concatenate(parts, axis=1)


def main_kernel(
    slots, latent_count, ring, sharers,
    indepartner_ref, own_ref, partner_ref, own_c_ref, partner_c_ref, whole_ref, query_ref,
    lat_ref, lat_c_ref, packed_ref,
    held_ref, arrived, weight_ref, grad_ref, total_ref, tail_ref,
):
    width_in = own_ref.shape[1]
    rows = own_ref.shape[0] - latent_count
    fetched = [
        pltpu.make_async_copy(ref, held_ref.at[n], arrived.at[n])
        for n, ref in enumerate((own_ref, partner_ref, own_c_ref, partner_c_ref))
    ]
    for copy in fetched:
        copy.start()
    capacity = rows // slots
    quarter = lat_ref.shape[2]
    head_size = quarter // HEADS
    scale = 1.0 / math.sqrt(head_size)
    strip = width_in // ring // 4
    for block in range(4):
        for part in range(4):
            strips = whole_ref[4 * part + block].astype(jnp.float32)
            for step in range(ring):
                start = strip * (4 * step + part)
                total_ref[start : start + strip, :] = strips[strip * step : strip * (step + 1)]
        weight_ref[:, LANES * block : LANES * (block + 1)] = total_ref[...].astype(jnp.bfloat16)
    first_head = iota((1, quarter), 1) < head_size
    nothing = jnp.zeros((), jnp.bfloat16)

    def head_of(array, head):
        return jnp.where(first_head, array, nothing) if head == 0 else jnp.where(first_head, nothing, array)

    def both_heads(array):
        return jnp.concatenate([head_of(array, 0), head_of(array, 1)], axis=0)

    width = query_ref.shape[1]
    pick = one_hot(
        (iota((width, 2 * LANES), 0) == quarter * indepartner_ref[0] + iota((width, 2 * LANES), 1))
        & (iota((width, 2 * LANES), 1) < quarter)
    )
    query = both_heads(plain(query_ref[...], pick).astype(jnp.bfloat16)[:, :quarter])
    tail_ref[...] = jnp.zeros_like(tail_ref)
    image_of = [
        sum((iota(shape, axis) >= capacity * n).astype(jnp.int32) for n in range(1, slots))
        for shape, axis in (((rows, 1), 0), ((1, rows), 1))
    ]
    place = [
        (iota(shape, axis) - capacity * image).astype(jnp.float32)
        for (shape, axis), image in zip((((rows, 1), 0), ((1, rows), 1)), image_of)
    ]
    members = [held_ref.at[n] for n in range(4)]
    first_pair = indepartner_ref[0] % 2 == 0
    outs = [ref.at[n] for ref in (lat_ref, lat_c_ref) for n in range(ref.shape[0])]
    apart = slots, capacity, HEADS * latent_count

    def limits(block):
        sizes = members[block][rows : rows + 16, 2 * quarter * slots :].astype(jnp.float32)
        size = [sizes[n : n + 1, 0:1] for n in range(slots)]
        live = []
        for image, position in zip(image_of, place):
            limit = size[slots - 1] + jnp.zeros_like(position)
            for n in reversed(range(slots - 1)):
                limit = jnp.where(image == n, size[n], limit)
            live.append(position < limit)
        return jnp.where(live[0], image_of[0], -1), jnp.where(live[1], image_of[1], -2)

    def attention(scores, allowed):
        scores = jnp.where(allowed, scores * scale, MASKED)
        highest = jnp.max(scores, axis=-1, keepdims=True)
        raised = jnp.exp(scores - highest)
        total = jnp.maximum(jnp.sum(raised, axis=-1, keepdims=True), 1.0)
        return (raised * (1.0 / total)).astype(jnp.bfloat16)

    def over_patches(scores, labels):
        inside = (labels[0] >= 0).reshape(slots, capacity, 1)
        masked = jnp.where(inside, scores.reshape(apart) * scale, MASKED)
        raised = jnp.where(inside, jnp.exp(masked - jnp.max(masked, axis=1, keepdims=True)), 0.0)
        return raised * (1.0 / jnp.maximum(jnp.sum(raised, axis=1, keepdims=True), 1.0))

    def normed(block):
        return members[block][:rows, :]

    def cotangent_of(block, n):
        ride = members[block][rows:, 2 * quarter * n : 2 * quarter * (n + 1)]
        return both_heads(jnp.where(first_pair, ride[:, :quarter], ride[:, quarter:]))

    def span(n):
        return slice(latent_count * n, latent_count * (n + 1))

    for copy in fetched:
        copy.wait()
    for first in range(0, len(members), WAVE):
        blocks = range(first, min(first + WAVE, len(members)))
        labels = [limits(b) for b in blocks]
        projected = [plain(normed(b), weight_ref[...]).astype(jnp.bfloat16) for b in blocks]
        parts = [
            [columns(p, quarter // 4, quarter * n, quarter * (n + 1)) for n in range(3)] for p in projected
        ]
        scores = [[across(head_of(q, h), k) for h in range(HEADS)] for q, k, _ in parts]
        weights = [[attention(s, m[0] == m[1]) for s in both] for both, m in zip(scores, labels)]
        mixed = [
            sum(plain(w[h], head_of(v, h)) for h in range(HEADS)).astype(jnp.bfloat16)
            for w, (_, _, v) in zip(weights, parts)
        ]
        shares = [over_patches(across(m, query), l) for m, l in zip(mixed, labels)]
        low = [s.astype(jnp.bfloat16) for s in shares]
        split = [m.reshape(slots, capacity, quarter) for m in mixed]
        cotangent = [[cotangent_of(b, n) for n in range(slots)] for b in blocks]
        share_grads = [
            jnp.stack([across(s[n], g[n]) for n in range(slots)]) for s, g in zip(split, cotangent)
        ]
        for b, l, s in zip(blocks, low, split):
            for n in range(slots):
                latents = along(l[n], s[n])
                outs[b][span(n), :] = jnp.where(first_head, latents[:latent_count], latents[latent_count:])
        score_grads = [
            s * (g - jnp.sum(s * g, axis=1, keepdims=True)) * scale for s, g in zip(shares, share_grads)
        ]
        score_grads = [g.reshape(rows, HEADS * latent_count) for g in score_grads]
        high = [g.astype(jnp.bfloat16) for g in score_grads]
        rest = [(g - h.astype(jnp.float32)).astype(jnp.bfloat16) for g, h in zip(score_grads, high)]
        from_values = [
            jnp.concatenate([plain(l[n], g[n]) for n in range(slots)], axis=0) for l, g in zip(low, cotangent)
        ]
        mixed_grad = [
            (v + (plain(h, query) + plain(r, query))).astype(jnp.bfloat16)
            for v, h, r in zip(from_values, high, rest)
        ]
        for b, w, g in zip(blocks, weights, mixed_grad):
            value_grad = sum(along(w[h], head_of(g, h)) for h in range(HEADS))
            grad_ref[rows * b : rows * (b + 1), :] = value_grad.astype(jnp.bfloat16)
    total = sum(
        along(grad_ref[rows * b : rows * (b + 1), :], normed(b)) for b in range(len(members))
    )
    total_ref[...] = total[:LANES].T
    tail_ref[:, : quarter - LANES] = total[LANES:].T
    depth = width_in // ring
    part = depth // sharers
    per_tile = LANES // (quarter - LANES)
    for sharer in range(sharers):
        rest = []
        for row in range(part):
            picked = pl.ds(sharer * part + row, ring, stride=depth)
            packed_ref[sharer, :, LANES * row : LANES * (row + 1)] = total_ref[picked, :].astype(jnp.bfloat16)
            tail = tail_ref[picked, :]
            shift = (row % per_tile) * (quarter - LANES)
            if shift == 0:
                rest.append(tail)
            else:
                rest[-1] = rest[-1] + pltpu.roll(tail, shift, 1)
        for n, tile in enumerate(rest):
            lanes = slice(LANES * (part + n), LANES * (part + n + 1))
            packed_ref[sharer, :, lanes] = tile.astype(jnp.bfloat16)


def order_kernel(indepartner_ref, own_ref, partner_ref, out_ref, parts_ref):
    quarter = own_ref.shape[2]
    parts_ref[:2] = own_ref[...]
    parts_ref[2:] = partner_ref[...]
    for pair in range(4):
        out_ref[:, quarter * pair : quarter * (pair + 1)] = parts_ref[pair ^ indepartner_ref[0]]


def call(kernel, outs, scratch, flops, *operands, limit=24, unplaced=()):
    memory = pl.BlockSpec(memory_space=pltpu.VMEM)
    scalars = pl.BlockSpec(memory_space=pltpu.SMEM)
    size = sum(math.prod(a.shape) * a.dtype.itemsize for a in (*operands, *outs))
    return pl.pallas_call(
        kernel,
        out_shape=outs,
        in_specs=[
            pl.BlockSpec(memory_space=pl.ANY) if n in unplaced else scalars if a.dtype == jnp.int32 else memory
            for n, a in enumerate(operands)
        ],
        out_specs=[memory] * len(outs),
        scratch_shapes=scratch,
        compiler_params=pltpu.CompilerParams(vmem_limit_bytes=limit * MIB),
        cost_estimate=pl.CostEstimate(flops=flops, bytes_accessed=size, transcendentals=0),
    )(*operands)


def pack(place, counts, images, grads):
    below = grads.shape[0] // counts.shape[0]
    send = jax.ShapeDtypeStruct((images.shape[0] + below, images.shape[1]), jnp.bfloat16)
    keep = jax.ShapeDtypeStruct((below, images.shape[1]), jnp.bfloat16)
    return call(pack_kernel, [send, keep], [], images.size, place, counts, images, grads, limit=56)


def layer_norm(rows, below, gain, bias):
    out = jax.ShapeDtypeStruct((rows.shape[0] + below.shape[0], rows.shape[1]), jnp.bfloat16)
    return call(norm_kernel, [out], [], 20 * rows.size, rows, below, gain, bias)[0]


def layer_norm_came(came, below, gain, bias):
    out = jax.ShapeDtypeStruct(came.shape, jnp.bfloat16)
    kernel = functools.partial(norm_came_kernel, below=below)
    return call(kernel, [out], [], 20 * came.size, came, gain, bias)[0]


def attend(index, members, whole, query, slots, latent_count, ring):
    width_in = members[0].shape[1]
    rows = members[0].shape[0] - latent_count
    quarter = query.shape[1] // 4
    sharers = whole.shape[0]
    part = width_in // ring // sharers
    packed = LANES * (part + -(-part * (quarter - LANES) // LANES))
    latents = jax.ShapeDtypeStruct((2, slots * latent_count, quarter), jnp.float32)
    return call(
        functools.partial(main_kernel, slots, latent_count, ring, sharers),
        [latents, latents, jax.ShapeDtypeStruct((sharers, ring, packed), jnp.bfloat16)],
        [
            pltpu.VMEM((4,) + members[0].shape, jnp.bfloat16),
            pltpu.SemaphoreType.DMA((4,)),
            pltpu.VMEM((width_in, 4 * LANES), jnp.bfloat16),
            pltpu.VMEM((4 * rows, quarter), jnp.bfloat16),
            pltpu.VMEM((width_in, LANES), jnp.float32),
            pltpu.VMEM((width_in, LANES), jnp.float32),
        ],
        2 * 4 * rows * width_in * 5 * quarter,
        index, *members, whole, query, unplaced=(1, 2, 3, 4), limit=56,
    )


def copies(piece, count):
    return jnp.broadcast_to(piece[None], (count,) + piece.shape)


def exchange(array, axes):
    return lax.all_to_all(array, axes, 0, 0, tiled=True)


def unpack(packed, part, quarter):
    lead = packed.shape[:-1]
    head = packed[..., : LANES * part].reshape(lead + (part, LANES))
    rest = packed[..., LANES * part : LANES * part + part * (quarter - LANES)]
    return jnp.concatenate([head, rest.reshape(lead + (part, quarter - LANES))], axis=-1)


def on_device(patches, counts, norm_gain, norm_bias, input_weight, latent_query, cotangent):
    slots, capacity, width_in = patches.shape[2:]
    latent_count, width = cotangent.shape[3:]
    depth = input_weight.shape[0]
    ring = lax.axis_size(RING)
    sharers = lax.axis_size(PLANE)
    x, y, c = (lax.axis_index(a) for a in DP)
    near_z = lax.axis_index("zl")
    pair = 2 * near_z + c
    quarter = width // 4

    images = patches.reshape(slots * capacity, width_in)
    grads = cotangent.reshape(slots * latent_count, width)
    send, keep = pack(near_z.astype(jnp.int32).reshape(1), counts.reshape(slots), images, grads)
    came = lax.ppermute(send, "zl", SWAP)

    piece = quarter // 4
    strip = depth // 4
    rows = lax.dynamic_slice_in_dim(input_weight, x * strip, strip, 0)
    target = jnp.arange(2 * LANES, dtype=jnp.int32)
    column = 3 * piece * y + target % LANES
    source = width * (column // quarter) + quarter * (2 * (target // LANES) + c) + column % quarter
    source = jnp.where(target % LANES < 3 * piece, source, -1)
    pick = (jnp.arange(3 * width, dtype=jnp.int32)[:, None] == source[None, :]).astype(jnp.bfloat16)
    own = jnp.dot(rows, pick, preferred_element_type=jnp.float32).astype(jnp.bfloat16)
    own = jnp.pad(jnp.stack([own[:, :LANES], own[:, LANES:]]), ((0, 0), (0, 4), (0, 0)))
    pieces = copies(own, ring // 2).reshape(ring, strip + 4, LANES)
    gathered = exchange(pieces, RING)

    own_rows = layer_norm(images, keep, norm_gain, norm_bias)
    own_c = lax.ppermute(own_rows, "c", SWAP)
    came_rows = layer_norm_came(came, keep.shape[0], norm_gain, norm_bias)
    came_c = lax.ppermute(came_rows, "c", SWAP)

    shape = jax.ShapeDtypeStruct((sharers, ring * strip, LANES), jnp.bfloat16)
    flat = pltpu.VMEM(shape.shape[1:], jnp.float32)
    whole = exchange(call(spread_kernel, [shape], [flat], gathered.size, gathered)[0], PLANE)
    index = pair.astype(jnp.int32).reshape(1)
    latents, latents_c, packed = attend(
        index, (own_rows, came_rows, own_c, came_c), whole, latent_query, slots, latent_count, ring
    )

    part = depth // sharers
    came = exchange(packed, PLANE)
    shape = jax.ShapeDtypeStruct((ring, 1, packed.shape[2]), jnp.float32)
    summed = call(plane_sum_kernel, [shape], [], came.size, came)[0]
    both = jnp.stack([latents, lax.ppermute(latents_c, "c", SWAP)], axis=1)
    summed = exchange(summed, RING)
    shape = jax.ShapeDtypeStruct((2 * sharers, 2, packed.shape[2]), jnp.float32)
    summed = call(ring_sum_kernel, [shape], [], summed.size, summed)[0]
    latents_z = lax.ppermute(both[1], "zl", SWAP)
    done = unpack(exchange(summed, DP), part, quarter)
    done = done.reshape(4, 4, 2, 2, part, quarter).transpose(0, 1, 4, 3, 2, 5)
    grad_value = done.reshape(depth, width)

    shape = jax.ShapeDtypeStruct((slots * latent_count, width), jnp.float32)
    parts = pltpu.VMEM((4,) + latents.shape[1:], jnp.float32)
    latents = call(order_kernel, [shape], [parts], both.size, index, both[0], latents_z)[0]
    return latents.reshape(cotangent.shape), grad_value


def solution(mesh):
    fine = Mesh(mesh.devices.reshape(4, 4, 2, 8, 2), DP + RING)
    placed = (
        P(DP, RING, None, None, None),
        P(DP, RING, None),
        P(),
        P(),
        P(RING, None),
        P(),
        P(DP, RING, None, None, None),
    )
    return jax.shard_map(
        on_device,
        mesh=fine,
        in_specs=placed,
        out_specs=(P(DP, RING, None, None, None), P(RING, None)),
        check_vma=False,
    )
```
